256 devices in a mesh: tmpl: 4 (over y_hi, core), row: 4 (over x), col: 16 (over z, y_lo).
Axes of the slice: x: 4, y: 4 (y_hi: 2, y_lo: 2; y = y_hi * 2 + y_lo), z: 8, core: 2. Of those that a mesh axis runs over, the one named last changes fastest.
Arguments:
- templ_pair: bfloat16 [4, 256, 256, 64], P('tmpl', 'row', 'col'), may hold values from -10 to 10
- main_pair: bfloat16 [256, 256, 128], P('row', 'col'), may hold values from -8 to 8
- coverage: int32 [4, 2], replicated, may hold values from 0 to 1
- pair_mask: int32 [2, 2], replicated, may hold values from 0 to 1
- tri_gain: float32 [64], replicated, may hold values from 0.1 to 1.9
- w_project: bfloat16 [64, 256], replicated, may hold values from -1 to 1
- w_bias: bfloat16 [64, 4], replicated, may hold values from -0.75 to 0.75
- w_tri_out: bfloat16 [64, 64], replicated, may hold values from -0.75 to 0.75
- merge_gain: float32 [64], replicated, may hold values from 0.1 to 1.9
- w_merge_q: bfloat16 [128, 64], replicated, may hold values from -1 to 1
- w_merge_kv: bfloat16 [64, 128], replicated, may hold values from -1 to 1
- w_merge_out: bfloat16 [64, 128], replicated, may hold values from -0.75 to 0.75
Outputs:
- templ_out: bfloat16 [4, 256, 256, 64], P('tmpl', 'row', 'col')
- embedding: bfloat16 [256, 256, 128], P('row', 'col')
The draws below stay inside these ranges and needn't reach their ends.
All inputs are finite; a program needn't handle non-finite values.
Results may differ from the reference program's by a relative error of at most 0.015.
Values may be sent and summed in bfloat16 or wider, within the bound.
A program may use at most 64 MiB of HBM per device.

```python
import jax
import jax.numpy as jnp
from jax import lax

TOKENS = 256
BLOCK = 128
TEMPL_CH = 64
PAIR_CH = 128
HEADS = 4
HEAD_DIM = 16
TEMPLATES = 4
NBLK = 2


def scaled_normal(key, tag, shape, fan_in):
    raw = jnp.clip(jax.random.normal(jax.random.fold_in(key, tag), shape, jnp.float32), -6.0, 6.0)
    return raw * fan_in ** (-0.5)


def draw_templ_pair(key, part):
    base = jnp.clip(jax.random.normal(jax.random.fold_in(key, 1), (TEMPLATES, TOKENS, TOKENS, TEMPL_CH), jnp.float32), -6.0, 6.0)
    return base.astype(jnp.bfloat16)


def draw_main_pair(key, part):
    base = jnp.clip(jax.random.normal(jax.random.fold_in(key, 2), (TOKENS, TOKENS, PAIR_CH), jnp.float32), -6.0, 6.0)
    return base.astype(jnp.bfloat16)


def draw_w_project(key, part):
    base = scaled_normal(key, 3, (TEMPL_CH, 4 * HEADS * HEAD_DIM), TEMPL_CH)
    return jnp.clip(base, -1.0, 1.0).astype(jnp.bfloat16)


def draw_w_merge_q(key, part):
    base = scaled_normal(key, 4, (PAIR_CH, HEADS * HEAD_DIM), PAIR_CH)
    return jnp.clip(base, -1.0, 1.0).astype(jnp.bfloat16)


def draw_w_merge_kv(key, part):
    base = scaled_normal(key, 5, (TEMPL_CH, 2 * HEADS * HEAD_DIM), TEMPL_CH)
    return jnp.clip(base, -1.0, 1.0).astype(jnp.bfloat16)


def place_ends(entries, stream_key, least, top_value):
    extent = entries.shape
    index_at = [jax.random.randint(jax.random.fold_in(stream_key, axis), (), 0, extent[axis]) for axis in range(len(extent))]
    entries = entries.at[tuple(index_at)].set(least)
    longest = extent.index(max(extent))
    index_at[longest] = (index_at[longest] + 1) % extent[longest]
    return entries.at[tuple(index_at)].set(top_value)


def bell_draw(stream_key, shape, scale, most, held_as=jnp.bfloat16):
    entries = jax.random.normal(stream_key, shape, jnp.float32) * scale
    return jnp.minimum(jnp.maximum(entries, -most), most).astype(held_as)


def setup_inputs(seed: int = 0) -> dict:
    streams_of = jax.random.split(jax.random.key(seed), 13)
    templ_pair = draw_templ_pair(jax.random.fold_in(streams_of[12], 71), 0)
    main_pair = draw_main_pair(jax.random.fold_in(streams_of[12], 71), 0)
    coverage = place_ends(jax.random.randint(streams_of[2], (TEMPLATES, NBLK), 0, 2), jax.random.fold_in(streams_of[2], 1), 0, 1).astype(jnp.int32)
    pair_mask = place_ends(jax.random.randint(streams_of[3], (NBLK, NBLK), 0, 2), jax.random.fold_in(streams_of[3], 1), 0, 1).astype(jnp.int32)
    tri_gain = jnp.clip(1.0 + 0.18 * jax.random.normal(streams_of[4], (TEMPL_CH,), jnp.float32), 0.1, 1.9)
    w_project = draw_w_project(jax.random.fold_in(streams_of[12], 71), 0)
    w_bias = bell_draw(streams_of[6], (TEMPL_CH, HEADS), TEMPL_CH ** -0.5, 0.75)
    w_tri_out = bell_draw(streams_of[7], (HEADS * HEAD_DIM, TEMPL_CH), (HEADS * HEAD_DIM) ** -0.5, 0.75)
    merge_gain = jnp.clip(1.0 + 0.18 * jax.random.normal(streams_of[8], (TEMPL_CH,), jnp.float32), 0.1, 1.9)
    w_merge_q = draw_w_merge_q(jax.random.fold_in(streams_of[12], 71), 0)
    w_merge_kv = draw_w_merge_kv(jax.random.fold_in(streams_of[12], 71), 0)
    w_merge_out = bell_draw(streams_of[11], (HEADS * HEAD_DIM, PAIR_CH), (HEADS * HEAD_DIM) ** -0.5, 0.75)
    return {"templ_pair": templ_pair, "main_pair": main_pair, "coverage": coverage, "pair_mask": pair_mask, "tri_gain": tri_gain, "w_project": w_project, "w_bias": w_bias, "w_tri_out": w_tri_out, "merge_gain": merge_gain, "w_merge_q": w_merge_q, "w_merge_kv": w_merge_kv, "w_merge_out": w_merge_out}


MASK_SHIFT = 10000.0
EPSILON = 1e-05

def layer_norm(values, scale_gain):
    values = values.astype(jnp.float32)
    center = values - lax.optimization_barrier(jnp.mean(values, axis=-1, keepdims=True))
    spread = lax.optimization_barrier(jnp.mean(center * center, axis=-1, keepdims=True))
    return center * lax.rsqrt(spread + EPSILON) * scale_gain

def reference(templ_pair, main_pair, coverage, pair_mask, tri_gain, w_project, w_bias, w_tri_out, merge_gain, w_merge_q, w_merge_kv, w_merge_out):
    hidden = HEADS * HEAD_DIM
    score_scale = HEAD_DIM ** (-0.5)
    channels = templ_pair.shape[-1]
    cover_tok = jnp.repeat(coverage, BLOCK, axis=1)
    pair_tok = jnp.repeat(jnp.repeat(pair_mask, BLOCK, axis=0), BLOCK, axis=1)
    valid_mask = cover_tok[:, :, None] * cover_tok[:, None, :] * pair_tok[None]
    shift_bias = MASK_SHIFT * (valid_mask.astype(jnp.float32) - 1.0)
    updated = []
    merge_rows = []
    for template in range(TEMPLATES):
        pair_tile = templ_pair[template]
        normed = layer_norm(pair_tile, tri_gain).astype(jnp.bfloat16)
        flat_norm = normed.reshape(-1, channels)
        project = jnp.dot(flat_norm, w_project, preferred_element_type=jnp.float32).reshape(TOKENS, TOKENS, 4 * hidden)
        queries = (project[..., :hidden] * score_scale).astype(jnp.bfloat16).reshape(TOKENS, TOKENS, HEADS, HEAD_DIM)
        keys_all = project[..., hidden:2 * hidden].astype(jnp.bfloat16).reshape(TOKENS, TOKENS, HEADS, HEAD_DIM)
        values_all = project[..., 2 * hidden:3 * hidden].astype(jnp.bfloat16).reshape(TOKENS, TOKENS, HEADS, HEAD_DIM)
        gate_values = jax.nn.sigmoid(project[..., 3 * hidden:])
        pair_bias = jnp.dot(flat_norm, w_bias, preferred_element_type=jnp.float32).astype(jnp.bfloat16)
        bias_head = jnp.transpose(pair_bias.reshape(TOKENS, TOKENS, HEADS), (0, 2, 1)).astype(jnp.float32)

        def one_row(row_args):
            query_row, key_row, value_row, shift_row = row_args
            scores = jnp.einsum('jhd,khd->jhk', query_row.astype(jnp.float32), key_row.astype(jnp.float32))
            scores = scores + bias_head + shift_row[None, None, :]
            highest = lax.optimization_barrier(jnp.max(scores, axis=-1, keepdims=True))
            weights = jnp.exp(scores - highest)
            totals = lax.optimization_barrier(jnp.sum(weights, axis=-1))
            rounded = weights.astype(jnp.bfloat16).astype(jnp.float32)
            summed = jnp.einsum('jhk,khd->jhd', rounded, value_row.astype(jnp.float32))
            return summed / totals[..., None]
        attended = lax.map(one_row, (queries, keys_all, values_all, shift_bias[template]))
        gated = (attended.reshape(TOKENS, TOKENS, hidden) * gate_values).astype(jnp.bfloat16)
        projected = jnp.dot(gated.reshape(-1, hidden), w_tri_out, preferred_element_type=jnp.float32).reshape(TOKENS, TOKENS, channels)
        new_pair = (pair_tile.astype(jnp.float32) + projected).astype(jnp.bfloat16)
        updated.append(new_pair)
        merge_norm = layer_norm(new_pair, merge_gain).astype(jnp.bfloat16)
        key_value = jnp.dot(merge_norm.reshape(-1, channels), w_merge_kv, preferred_element_type=jnp.float32).astype(jnp.bfloat16)
        merge_rows.append(key_value.reshape(TOKENS, TOKENS, 2 * hidden))
    merge_kv = jnp.stack(merge_rows)
    pair_ch = main_pair.shape[-1]
    main_query = (jnp.dot(main_pair.reshape(-1, pair_ch), w_merge_q, preferred_element_type=jnp.float32) * score_scale).reshape(TOKENS, TOKENS, HEADS, HEAD_DIM)
    merge_keys = merge_kv[..., :hidden].astype(jnp.float32).reshape(TEMPLATES, TOKENS, TOKENS, HEADS, HEAD_DIM)
    merge_values = merge_kv[..., hidden:].astype(jnp.float32).reshape(TEMPLATES, TOKENS, TOKENS, HEADS, HEAD_DIM)
    merge_scores = jnp.einsum('ijhd,tijhd->tijh', main_query, merge_keys) + shift_bias[..., None]
    highest = lax.optimization_barrier(jnp.max(merge_scores, axis=0, keepdims=True))
    weights = jnp.exp(merge_scores - highest)
    totals = lax.optimization_barrier(jnp.sum(weights, axis=0))
    merged = jnp.einsum('tijh,tijhd->ijhd', weights, merge_values) / totals[..., None]
    merged = merged.reshape(-1, hidden).astype(jnp.bfloat16)
    embedding = jnp.dot(merged, w_merge_out, preferred_element_type=jnp.float32).astype(jnp.bfloat16).reshape(TOKENS, TOKENS, pair_ch)
    return (jnp.stack(updated), embedding)
```

```python
import jax
import jax.numpy as jnp
from jax import lax
from jax.experimental import pallas as pl
from jax.experimental.pallas import tpu as pltpu
from jax.sharding import PartitionSpec as P

MASK_SHIFT = 10000.0
EPSILON = 1e-05
MESH = pl.DeviceIdType.MESH
F32 = jnp.float32
BF16 = jnp.bfloat16


def iota(shape, axis):
    return lax.broadcasted_iota(jnp.int32, shape, axis)


def dot_nn(a, b):
    return lax.dot_general(a, b, (((1,), (0,)), ((), ())), preferred_element_type=F32)


def dot_nt(a, b):
    return lax.dot_general(a, b, (((1,), (1,)), ((), ())), preferred_element_type=F32)


def dot_tn(a, b):
    return lax.dot_general(a, b, (((0,), (0,)), ((), ())), preferred_element_type=F32)


def split_dot(values, weights):
    high = values.astype(BF16)
    low = (values - high.astype(F32)).astype(BF16)
    return dot_nn(high, weights) + dot_nn(low, weights)


def pair_norm(values, averager, gain):
    center = values.astype(F32) - dot_nn(values, averager)
    spread = split_dot(center * center, averager)
    return (center * lax.rsqrt(spread + EPSILON) * gain).astype(BF16)


def ones_where(condition):
    return jnp.where(condition, 1.0, 0.0).astype(BF16)


def diagonal(doubled):
    both = jnp.concatenate([doubled, doubled], axis=0)
    keep = (iota((128, 128), 0) < 64) == (iota((128, 128), 1) < 64)
    return jnp.where(keep, both, 0.0).astype(BF16)


def pick_columns(width, first):
    return ones_where(iota((width, 128), 0) == first + iota((width, 128), 1) % 64)


def pair_kernel(
    templ_ref,
    main_ref,
    coverage_ref,
    mask_ref,
    tri_gain_ref,
    w_project_ref,
    w_bias_ref,
    w_tri_ref,
    merge_gain_ref,
    w_query_ref,
    w_kv_ref,
    new_out,
    merged_out,
    tile,
    packed,
    rows_in,
    bias_tile,
    bias_in,
    bias_full,
    main_in,
    normed,
    fresh,
    peers_in,
    merged,
    sizes,
    load_sem,
    rows_send,
    rows_recv,
    bias_send,
    bias_recv,
    main_send,
    main_recv,
    peer_send,
    peer_recv,
    new_send,
    new_recv,
    merged_send,
    merged_recv,
    second_sem,
):
    templ = lax.axis_index("tmpl")
    row = lax.axis_index("row")
    col = lax.axis_index("col")
    plane, half = col // 2, col % 2
    col_half = col // 8

    load = pltpu.make_async_copy(templ_ref, tile, load_sem)
    load.start()

    barrier = pltpu.get_barrier_semaphore()
    for step in range(1, 16):
        pl.semaphore_signal(barrier, inc=1, device_id=(templ, row, (col + step) % 16), device_id_type=MESH)
    for step in range(1, 4):
        pl.semaphore_signal(barrier, inc=1, device_id=(templ, (row + step) % 4, col), device_id_type=MESH)
        pl.semaphore_signal(barrier, inc=1, device_id=((templ + step) % 4, row, col), device_id_type=MESH)

    load.wait()
    eye = iota((64, 128), 0)
    lane = iota((64, 128), 1)
    low_rows = tile[pl.ds(0, 32)].reshape(512, 64)
    high_rows = tile[pl.ds(32, 32)].reshape(512, 64)
    together = dot_nn(low_rows, ones_where(eye == lane)) + dot_nn(high_rows, ones_where(eye + 64 == lane))
    packed[...] = together.astype(BF16).reshape(32, 16, 128)

    pl.semaphore_wait(barrier, 21)
    for step in range(1, 4):
        pl.semaphore_signal(second_sem, inc=1, device_id=(templ, (row + step) % 4, col), device_id_type=MESH)
        pl.semaphore_signal(second_sem, inc=1, device_id=((templ + step) % 4, row, col), device_id_type=MESH)

    own_rows = pltpu.make_async_copy(
        packed.at[pl.ds(4 * plane, 4)], rows_in.at[:, pl.ds(pl.multiple_of(16 * col, 16), 16), :], rows_recv
    )
    own_rows.start()

    def send_rows(step, carry):
        to = (col + step) % 16
        pltpu.make_async_remote_copy(
            src_ref=packed.at[pl.ds(4 * (to // 2), 4)],
            dst_ref=rows_in.at[:, pl.ds(pl.multiple_of(16 * col, 16), 16), :],
            send_sem=rows_send,
            recv_sem=rows_recv,
            device_id=(templ, row, to),
            device_id_type=MESH,
        ).start()
        return carry

    lax.fori_loop(1, 16, send_rows, 0)

    averager = jnp.where(
        (iota((128, 128), 0) < 64) == (iota((128, 128), 1) < 64), 1.0 / 64, 0.0
    ).astype(BF16)
    tri_gain = jnp.concatenate([tri_gain_ref[...], tri_gain_ref[...]], axis=1)
    own_normed = pair_norm(packed[...].reshape(512, 128), averager, tri_gain)

    w_bias = dot_nn(w_bias_ref[...], pick_columns(64, 0))
    which = iota((256, 128), 0)
    spread_bias = jnp.zeros((256, 128), F32)
    for head in range(4):
        spread_bias = jnp.where(which // 64 == head, w_bias[head : head + 1, :], spread_bias)
    spread_bias = jnp.where((which // 32) % 2 == iota((256, 128), 1) // 64, spread_bias, 0.0).astype(BF16)
    every_bias = dot_nt(own_normed, spread_bias).reshape(32, 16, 256)
    place = iota((16, 256), 1) % 32
    chosen = jnp.zeros((16, 256), F32)
    for index in range(32):
        chosen = jnp.where(place == index, every_bias[index], chosen)
    chosen = chosen.astype(BF16)
    bias_tile[0] = chosen[:, :128]
    bias_tile[1] = chosen[:, 128:]

    pl.semaphore_wait(second_sem, 6)
    bias_half = row // 2

    def bias_place():
        return bias_in.at[row % 2, :, pl.ds(pl.multiple_of(16 * col, 16), 16), :]

    def send_bias(step, carry):
        to_row, to_plane = (row + step) % 4, (plane + step // 4) % 8
        to_col = 2 * to_plane + bias_half
        here = (to_row == row) & (to_col == col)

        @pl.when(here)
        def _():
            pltpu.make_async_copy(bias_tile, bias_place(), bias_recv).start()

        @pl.when(jnp.logical_not(here))
        def _():
            pltpu.make_async_remote_copy(
                src_ref=bias_tile,
                dst_ref=bias_place(),
                send_sem=bias_send,
                recv_sem=bias_recv,
                device_id=(templ, to_row, to_col),
                device_id_type=MESH,
            ).start()

        return carry

    lax.fori_loop(0, 32, send_bias, 0)

    def main_place():
        return main_in.at[:, pl.ds(pl.multiple_of(16 * (col % 8), 16), 16), :]

    def send_main(step, carry):
        to_plane = (plane + step) % 8
        to_col = 2 * to_plane + col_half
        here = to_col == col
        source = main_ref.at[:, 4 * to_plane + templ]

        @pl.when(here)
        def _():
            pltpu.make_async_copy(source, main_place(), main_recv).start()

        @pl.when(jnp.logical_not(here))
        def _():
            pltpu.make_async_remote_copy(
                src_ref=source,
                dst_ref=main_place(),
                send_sem=main_send,
                recv_sem=main_recv,
                device_id=(templ, row, to_col),
                device_id_type=MESH,
            ).start()

        return carry

    lax.fori_loop(0, 8, send_main, 0)

    w_project = w_project_ref[...]
    double = pick_columns(64, 0)

    def turned(first):
        columns = ones_where(iota((128, 256), 1) == first + iota((128, 256), 0) % 64)
        wide = dot_nn(dot_nt(columns, w_project).astype(BF16), double)
        keep = (iota((128, 128), 0) < 64) == (iota((128, 128), 1) < 64)
        return jnp.where(keep, wide, 0.0).astype(BF16)

    turned_query, turned_value, turned_gate = turned(0), turned(128), turned(192)
    w_key = diagonal(dot_nn(w_project, pick_columns(256, 64)))
    w_tri = diagonal(dot_nn(w_tri_ref[...], double))
    ones_rows = jnp.ones((16, 256), BF16)
    head_of = iota((128, 128), 0) // 16

    row_block = row // 2
    cover_row = coverage_ref[row_block, templ]
    shift_low = MASK_SHIFT * ((cover_row * coverage_ref[0, templ] * mask_ref[row_block, 0]).astype(F32) - 1.0)
    shift_high = MASK_SHIFT * ((cover_row * coverage_ref[1, templ] * mask_ref[row_block, 1]).astype(F32) - 1.0)
    gap = shift_high - shift_low

    pltpu.make_async_copy(bias_in, bias_in, bias_recv).wait()
    first_half = iota((256, 128), 1) < 64
    for pair in range(2):
        one = bias_in[0, pair].astype(F32)
        two = bias_in[1, pair].astype(F32)
        bias_full[2 * pair] = jnp.where(first_half, one, pltpu.roll(two, 64, 1))
        bias_full[2 * pair + 1] = jnp.where(first_half, pltpu.roll(one, 64, 1), two)

    pltpu.make_async_copy(rows_in, rows_in, rows_recv).wait()
    mine = pl.ds(pl.multiple_of(128 * half, 128), 128)

    def attend(step, carry):
        pair = (templ + 1 + step) % 4
        normed_all = pair_norm(rows_in[pair], averager, tri_gain)
        normed[...] = normed_all
        keys = dot_nn(normed_all, w_key).astype(BF16)
        values = dot_nt(turned_value, normed_all).astype(BF16)
        normed_mine = normed[mine, :]
        queries = (dot_nt(turned_query, normed_mine) * 0.25).astype(BF16)
        gates = jax.nn.sigmoid(dot_nt(turned_gate, normed_mine))
        parts = []
        for index in range(8):
            alone = jnp.where(head_of == index, queries, jnp.zeros_like(queries))
            scores = dot_nn(keys, alone) + bias_full[index % 4]
            low, high = scores[:128], scores[128:]
            top_low = jnp.max(low, axis=0, keepdims=True)
            top_high = jnp.max(high, axis=0, keepdims=True)
            weights = jnp.concatenate(
                [
                    jnp.exp(low - jnp.maximum(top_low, top_high + gap)),
                    jnp.exp(high - jnp.maximum(top_low - gap, top_high)),
                ],
                axis=0,
            ).astype(BF16)
            mixed = dot_nn(
                jnp.concatenate([values[16 * index : 16 * index + 16], ones_rows], axis=0), weights
            )
            parts.append(mixed[:16] / mixed[16:])
        gated = (jnp.concatenate(parts, axis=0) * gates).astype(BF16)
        projected = dot_tn(gated, w_tri)
        result = (rows_in[pair, mine, :].astype(F32) + projected).astype(BF16)
        fresh[pair] = result

        @pl.when(pair == templ)
        def _():
            peers_in[templ] = result

        @pl.when(pair != templ)
        def _():
            pltpu.make_async_remote_copy(
                src_ref=fresh.at[pair],
                dst_ref=peers_in.at[templ],
                send_sem=peer_send.at[step],
                recv_sem=peer_recv.at[templ],
                device_id=(pair, row, col),
                device_id_type=MESH,
            ).start()

        def send_new(index, inner):
            to_col = 8 * half + (col + index) % 8
            source = fresh.at[pair, pl.ds(pl.multiple_of(16 * ((col + index) % 8), 16), 16), :]

            @pl.when(to_col == col)
            def _():
                pltpu.make_async_copy(source, new_out.at[4 * plane + pair], new_recv).start()

            @pl.when(to_col != col)
            def _():
                pltpu.make_async_remote_copy(
                    src_ref=source,
                    dst_ref=new_out.at[4 * plane + pair],
                    send_sem=new_send,
                    recv_sem=new_recv,
                    device_id=(templ, row, to_col),
                    device_id_type=MESH,
                ).start()

            return inner

        lax.fori_loop(0, 8, send_new, 0)
        return carry

    lax.fori_loop(0, 4, attend, 0)

    pltpu.make_async_copy(main_in, main_in, main_recv).wait()
    w_query = w_query_ref[...]
    nothing = jnp.zeros_like(w_query)
    main_query = 0.25 * (
        dot_nt(main_in[0], jnp.concatenate([w_query, nothing], axis=0))
        + dot_nt(main_in[1], jnp.concatenate([nothing, w_query], axis=0))
    )
    w_kv = w_kv_ref[...]
    w_merge_key = diagonal(dot_nn(w_kv, pick_columns(128, 0)))
    w_merge_value = diagonal(dot_nn(w_kv, pick_columns(128, 64)))
    merge_gain = jnp.concatenate([merge_gain_ref[...], merge_gain_ref[...]], axis=1)
    summer = ones_where(iota((128, 128), 0) // 16 == iota((128, 128), 1) // 16)

    def wait_peer(step, carry):
        source = (templ + step) % 4
        pltpu.make_async_copy(peers_in.at[source], peers_in.at[source], peer_recv.at[source]).wait()
        return carry

    lax.fori_loop(1, 4, wait_peer, 0)
    scores = []
    shown = []
    for other in range(4):
        other_normed = pair_norm(peers_in[other], averager, merge_gain)
        merge_keys = dot_nn(other_normed, w_merge_key).astype(BF16).astype(F32)
        shown.append(dot_nn(other_normed, w_merge_value).astype(BF16).astype(F32))
        valid = coverage_ref[row_block, other] * coverage_ref[half, other] * mask_ref[row_block, half]
        scores.append(split_dot(main_query * merge_keys, summer) + MASK_SHIFT * (valid.astype(F32) - 1.0))
    highest = jnp.maximum(jnp.maximum(scores[0], scores[1]), jnp.maximum(scores[2], scores[3]))
    weights = [jnp.exp(score - highest) for score in scores]
    total = (weights[0] + weights[1]) + (weights[2] + weights[3])
    blend = (weights[0] * shown[0] + weights[1] * shown[1]) + (weights[2] * shown[2] + weights[3] * shown[3])
    merged[...] = (blend / total).astype(BF16)

    def send_merged(step, carry):
        to_templ = (templ + step) % 4
        to_col = 8 * half + (col + step // 4) % 8
        here = (to_templ == templ) & (to_col == col)
        source = merged.at[pl.ds(pl.multiple_of(16 * ((col + step // 4) % 8), 16), 16), :]

        @pl.when(here)
        def _():
            pltpu.make_async_copy(source, merged_out.at[4 * plane + templ], merged_recv).start()

        @pl.when(jnp.logical_not(here))
        def _():
            pltpu.make_async_remote_copy(
                src_ref=source,
                dst_ref=merged_out.at[4 * plane + templ],
                send_sem=merged_send,
                recv_sem=merged_recv,
                device_id=(to_templ, row, to_col),
                device_id_type=MESH,
            ).start()

        return carry

    lax.fori_loop(0, 32, send_merged, 0)

    def drain(ref, sem):
        pltpu.make_async_copy(ref, ref, sem).wait()

    for step in range(3):
        drain(fresh.at[0], peer_send.at[step])
    drain(sizes.at[pl.ds(0, 30)], rows_send)
    to_self = col_half == half

    @pl.when(bias_half == half)
    def _():
        drain(sizes.at[pl.ds(0, 31)], bias_send)

    @pl.when(bias_half != half)
    def _():
        drain(sizes.at[pl.ds(0, 32)], bias_send)

    @pl.when(to_self)
    def _():
        drain(sizes.at[pl.ds(0, 7)], main_send)
        drain(sizes.at[pl.ds(0, 14)], new_send)
        drain(packed.at[pl.ds(0, 31)], merged_send)

    @pl.when(jnp.logical_not(to_self))
    def _():
        drain(sizes.at[pl.ds(0, 8)], main_send)
        drain(sizes.at[pl.ds(0, 16)], new_send)
        drain(packed.at[pl.ds(0, 32)], merged_send)

    drain(new_out, new_recv)
    drain(merged_out, merged_recv)


def out_kernel(new_ref, merged_ref, w_out_ref, templ_ref, embedding_ref):
    new = new_ref[...]
    templ_ref[0, pl.ds(0, 32)] = new[:, :, :64]
    templ_ref[0, pl.ds(32, 32)] = new[:, :, 64:]
    merged = merged_ref[...].reshape(512, 128)
    w_out = w_out_ref[...]
    nothing = jnp.zeros_like(w_out)
    first = dot_nn(merged, jnp.concatenate([w_out, nothing], axis=0))
    second = dot_nn(merged, jnp.concatenate([nothing, w_out], axis=0))
    embedding_ref[pl.ds(0, 32)] = first.astype(BF16).reshape(32, 16, 128)
    embedding_ref[pl.ds(32, 32)] = second.astype(BF16).reshape(32, 16, 128)


def on_device(
    templ_pair,
    main_pair,
    coverage,
    pair_mask,
    tri_gain,
    w_project,
    w_bias,
    w_tri_out,
    merge_gain,
    w_merge_q,
    w_merge_kv,
    w_merge_out,
):
    vmem = pl.BlockSpec(memory_space=pltpu.VMEM)
    smem = pl.BlockSpec(memory_space=pltpu.SMEM)
    anywhere = pl.BlockSpec(memory_space=pl.ANY)
    piece = jax.ShapeDtypeStruct((32, 16, 128), BF16)
    dma = pltpu.SemaphoreType.DMA
    new, merged = pl.pallas_call(
        pair_kernel,
        out_shape=(piece, piece),
        in_specs=[anywhere, anywhere, smem, smem] + [vmem] * 7,
        out_specs=(anywhere, anywhere),
        scratch_shapes=[
            pltpu.VMEM((64, 16, 64), BF16),
            pltpu.VMEM((32, 16, 128), BF16),
            pltpu.VMEM((4, 256, 128), BF16),
            pltpu.VMEM((2, 16, 128), BF16),
            pltpu.VMEM((2, 2, 256, 128), BF16),
            pltpu.VMEM((4, 256, 128), F32),
            pltpu.VMEM((2, 128, 128), BF16),
            pltpu.VMEM((256, 128), BF16),
            pltpu.VMEM((4, 128, 128), BF16),
            pltpu.VMEM((4, 128, 128), BF16),
            pltpu.VMEM((128, 128), BF16),
            pltpu.VMEM((32, 16, 256), BF16),
            dma,
            dma,
            dma,
            dma,
            dma,
            dma,
            dma,
            dma((4,)),
            dma((4,)),
            dma,
            dma,
            dma,
            dma,
            pltpu.SemaphoreType.REGULAR,
        ],
        compiler_params=pltpu.CompilerParams(
            collective_id=0, has_side_effects=True, vmem_limit_bytes=40 * 1024 * 1024
        ),
        name="pair_kernel",
    )(
        templ_pair[0],
        main_pair.reshape(2, 32, 16, 128),
        coverage.T,
        pair_mask,
        tri_gain.reshape(1, 64),
        w_project,
        w_bias.T,
        w_tri_out,
        merge_gain.reshape(1, 64),
        w_merge_q.T,
        w_merge_kv,
    )
    return pl.pallas_call(
        out_kernel,
        out_shape=(
            jax.ShapeDtypeStruct((1, 64, 16, 64), BF16),
            jax.ShapeDtypeStruct((64, 16, 128), BF16),
        ),
        in_specs=[vmem] * 3,
        out_specs=(vmem, vmem),
        compiler_params=pltpu.CompilerParams(vmem_limit_bytes=40 * 1024 * 1024),
        name="out_kernel",
    )(new, merged, w_merge_out)


def solution(mesh):
    whole = P()
    tiles = P("tmpl", "row", "col", None)
    pairs = P("row", "col", None)
    return jax.shard_map(
        on_device,
        mesh=mesh,
        in_specs=(tiles, pairs) + (whole,) * 10,
        out_specs=(tiles, pairs),
        check_vma=False,
    )
```

```python
import jax
import jax.numpy as jnp
from jax import lax
from jax.experimental import pallas as pl
from jax.experimental.pallas import tpu as pltpu
from jax.sharding import PartitionSpec as P

MASK_SHIFT = 10000.0
EPSILON = 1e-05
MESH = pl.DeviceIdType.MESH
F32 = jnp.float32
BF16 = jnp.bfloat16


def iota(shape, axis):
    return lax.broadcasted_iota(jnp.int32, shape, axis)


def dot_nn(a, b):
    return lax.dot_general(a, b, (((1,), (0,)), ((), ())), preferred_element_type=F32)


def dot_nt(a, b):
    return lax.dot_general(a, b, (((1,), (1,)), ((), ())), preferred_element_type=F32)


def dot_tn(a, b):
    return lax.dot_general(a, b, (((0,), (0,)), ((), ())), preferred_element_type=F32)


def split_dot(values, weights):
    high = values.astype(BF16)
    low = (values - high.astype(F32)).astype(BF16)
    return dot_nn(high, weights) + dot_nn(low, weights)


def pair_norm(values, averager, gain):
    center = values.astype(F32) - dot_nn(values, averager)
    spread = split_dot(center * center, averager)
    return (center * lax.rsqrt(spread + EPSILON) * gain).astype(BF16)


def ones_where(condition):
    return jnp.where(condition, 1.0, 0.0).astype(BF16)


def diagonal(doubled):
    both = jnp.concatenate([doubled, doubled], axis=0)
    keep = (iota((128, 128), 0) < 64) == (iota((128, 128), 1) < 64)
    return jnp.where(keep, both, 0.0).astype(BF16)


def pick_columns(width, first):
    return ones_where(iota((width, 128), 0) == first + iota((width, 128), 1) % 64)


def pair_kernel(
    templ_hbm,
    main_hbm,
    coverage_hbm,
    mask_hbm,
    tri_gain_hbm,
    w_project_hbm,
    w_bias_hbm,
    w_tri_hbm,
    merge_gain_hbm,
    w_query_hbm,
    w_kv_hbm,
    new_out,
    merged_out,
    tile,
    coverage_ref,
    mask_ref,
    tri_gain_ref,
    w_project_ref,
    w_bias_ref,
    w_tri_ref,
    merge_gain_ref,
    w_query_ref,
    w_kv_ref,
    packed,
    rows_in,
    bias_rows,
    bias_in,
    bias_full,
    main_in,
    normed,
    keys,
    values,
    queries,
    gates,
    scores,
    gated,
    fresh,
    peers_in,
    merged,
    sizes,
    load_sem,
    rows_send,
    rows_recv,
    cross_send,
    cross_recv,
    bias_send,
    bias_recv,
    main_send,
    main_recv,
    peer_send,
    peer_recv,
    new_send,
    new_recv,
    merged_send,
    merged_recv,
    second_sem,
):
    templ = lax.axis_index("tmpl")
    row = lax.axis_index("row")
    col = lax.axis_index("col")
    plane = col // 2
    half, chunk = col // 8, col % 8
    own_cols = pl.ds(pl.multiple_of(16 * col, 16), 16)

    loads = [
        pltpu.make_async_copy(source, target, load_sem.at[index])
        for index, (source, target) in enumerate(
            (
                (templ_hbm, tile),
                (tri_gain_hbm, tri_gain_ref),
                (w_bias_hbm, w_bias_ref),
                (w_project_hbm, w_project_ref),
                (w_tri_hbm, w_tri_ref),
                (merge_gain_hbm, merge_gain_ref),
                (w_query_hbm, w_query_ref),
                (w_kv_hbm, w_kv_ref),
                (coverage_hbm, coverage_ref),
                (mask_hbm, mask_ref),
            )
        )
    ]
    barrier = pltpu.get_barrier_semaphore()
    for step in range(1, 16):
        pl.semaphore_signal(barrier, inc=1, device_id=(templ, row, (col + step) % 16), device_id_type=MESH)
    for step in range(1, 4):
        pl.semaphore_signal(barrier, inc=1, device_id=(templ, (row + step) % 4, col), device_id_type=MESH)
        pl.semaphore_signal(barrier, inc=1, device_id=((templ + step) % 4, row, col), device_id_type=MESH)
    for load in loads:
        load.start()

    for load in loads[:3]:
        load.wait()
    eye = iota((64, 128), 0)
    lane = iota((64, 128), 1)
    low_rows = tile[pl.ds(0, 32)].reshape(512, 64)
    high_rows = tile[pl.ds(32, 32)].reshape(512, 64)
    together = dot_nn(low_rows, ones_where(eye == lane)) + dot_nn(high_rows, ones_where(eye + 64 == lane))
    packed[...] = together.astype(BF16).reshape(32, 16, 128)

    averager = jnp.where(
        (iota((128, 128), 0) < 64) == (iota((128, 128), 1) < 64), 1.0 / 64, 0.0
    ).astype(BF16)
    tri_gain = jnp.concatenate([tri_gain_ref[...], tri_gain_ref[...]], axis=1)

    pl.semaphore_wait(barrier, 21)
    for step in range(1, 4):
        pl.semaphore_signal(second_sem, inc=1, device_id=((templ + step) % 4, row, col), device_id_type=MESH)

    def far_first(index):
        away = (index // 2 + 1) // 2 * (2 * (index // 2 % 2) - 1)
        return 2 * ((plane + 4 + away) % 8) + (col + index) % 2

    def send_to_columns(source_of, target, local_target, send_sem, recv_sem):
        def one(index, carry):
            to = far_first(index)
            pltpu.make_async_remote_copy(
                src_ref=source_of(to),
                dst_ref=target,
                send_sem=send_sem,
                recv_sem=recv_sem,
                device_id=(templ, row, to),
                device_id_type=MESH,
            ).start()
            return carry

        lax.fori_loop(0, 14, one, 0)
        one(15, 0)
        pltpu.make_async_copy(source_of(col), local_target, recv_sem).start()

    rows_place = rows_in.at[:, own_cols, :]
    send_to_columns(
        lambda to: packed.at[pl.ds(4 * (to % 8), 4)], rows_place, rows_place, rows_send, rows_recv
    )

    own_normed = pair_norm(packed[...].reshape(512, 128), averager, tri_gain)
    w_bias = dot_nn(w_bias_ref[...], pick_columns(64, 0))
    which = iota((256, 128), 0)
    spread_bias = jnp.zeros((256, 128), F32)
    for head in range(4):
        spread_bias = jnp.where(which // 64 == head, w_bias[head : head + 1, :], spread_bias)
    spread_bias = jnp.where((which // 32) % 2 == iota((256, 128), 1) // 64, spread_bias, 0.0).astype(BF16)
    every_bias = dot_nt(own_normed, spread_bias).reshape(32, 16, 256)
    place = iota((16, 256), 1) % 32
    chosen = jnp.zeros((16, 256), F32)
    for index in range(32):
        chosen = jnp.where(place == index, every_bias[index], chosen)
    chosen = chosen.astype(BF16)
    bias_rows[0, row] = chosen[:, :128]
    bias_rows[1, row] = chosen[:, 128:]

    for step in range(1, 4):
        pltpu.make_async_remote_copy(
            src_ref=bias_rows.at[:, row],
            dst_ref=bias_rows.at[:, row],
            send_sem=cross_send,
            recv_sem=cross_recv,
            device_id=(templ, (row + step) % 4, col),
            device_id_type=MESH,
        ).start()

    for load in loads[3:]:
        load.wait()
    w_project = w_project_ref[...]
    double = pick_columns(64, 0)

    def turned(first):
        columns = ones_where(iota((128, 256), 1) == first + iota((128, 256), 0) % 64)
        wide = dot_nn(dot_nt(columns, w_project).astype(BF16), double)
        keep = (iota((128, 128), 0) < 64) == (iota((128, 128), 1) < 64)
        return jnp.where(keep, wide, 0.0).astype(BF16)

    turned_query, turned_value, turned_gate = turned(0), turned(128), turned(192)
    w_key = diagonal(dot_nn(w_project, pick_columns(256, 64)))
    w_tri = diagonal(dot_nn(w_tri_ref[...], double))
    ones_rows = jnp.ones((16, 256), BF16)
    head_of = iota((128, 128), 0) // 16

    w_query = w_query_ref[...]
    nothing = jnp.zeros_like(w_query)
    w_kv = w_kv_ref[...]
    w_merge_key = diagonal(dot_nn(w_kv, pick_columns(128, 0)))
    w_merge_value = diagonal(dot_nn(w_kv, pick_columns(128, 64)))
    merge_gain = jnp.concatenate([merge_gain_ref[...], merge_gain_ref[...]], axis=1)
    summer = ones_where(iota((128, 128), 0) // 16 == iota((128, 128), 1) // 16)

    def drain(ref, sem):
        pltpu.make_async_copy(ref, ref, sem).wait()

    drain(sizes.at[pl.ds(0, 3)], cross_recv)
    for heads in range(2):
        bias_place = bias_in.at[heads, :, own_cols, :]
        send_to_columns(
            lambda to, heads=heads: bias_rows.at[heads, pl.ds(2 * (to // 8), 2)],
            bias_place,
            bias_place,
            bias_send.at[heads],
            bias_recv.at[heads],
        )

    main_place = main_in.at[:, pl.ds(pl.multiple_of(16 * chunk, 16), 16), :]
    pltpu.make_async_copy(main_hbm.at[:, 4 * chunk + templ], main_place, main_recv).start()

    def send_main(step, carry):
        to_chunk = (chunk + step) % 8
        pltpu.make_async_remote_copy(
            src_ref=main_hbm.at[:, 4 * to_chunk + templ],
            dst_ref=main_place,
            send_sem=main_send,
            recv_sem=main_recv,
            device_id=(templ, row, 8 * half + to_chunk),
            device_id_type=MESH,
        ).start()
        return carry

    lax.fori_loop(1, 8, send_main, 0)

    row_block = row // 2
    cover_row = coverage_ref[row_block, templ]
    shift_low = MASK_SHIFT * ((cover_row * coverage_ref[0, templ] * mask_ref[row_block, 0]).astype(F32) - 1.0)
    shift_high = MASK_SHIFT * ((cover_row * coverage_ref[1, templ] * mask_ref[row_block, 1]).astype(F32) - 1.0)
    gap = shift_high - shift_low
    mine = pl.ds(pl.multiple_of(128 * half, 128), 128)

    drain(rows_in, rows_recv)
    every_normed = pair_norm(rows_in[...].reshape(1024, 128), averager, tri_gain)
    normed[...] = every_normed.reshape(4, 256, 128)
    keys[...] = dot_nn(every_normed, w_key).astype(BF16).reshape(4, 256, 128)
    every_value = dot_nt(turned_value, every_normed).astype(BF16)
    own_part = normed[:, mine, :].reshape(512, 128)
    every_query = (dot_nt(turned_query, own_part) * 0.25).astype(BF16)
    every_gate = jax.nn.sigmoid(dot_nt(turned_gate, own_part))
    for pair in range(4):
        values[pair] = every_value[:, 256 * pair : 256 * pair + 256]
        queries[pair] = every_query[:, 128 * pair : 128 * pair + 128]
        gates[pair] = every_gate[:, 128 * pair : 128 * pair + 128]

    def score(pair, carry):
        pair_keys, pair_queries = keys[pair], queries[pair]
        nothing = jnp.zeros_like(pair_queries)
        for index in range(4):
            two_heads = jnp.concatenate(
                [
                    jnp.where(head_of == 2 * index, pair_queries, nothing),
                    jnp.where(head_of == 2 * index + 1, pair_queries, nothing),
                ],
                axis=1,
            )
            scores[pair, index] = dot_nn(pair_keys, two_heads)
        return carry

    lax.fori_loop(0, 4, score, 0)

    def soft(values, bias):
        values = values + bias
        low, high = values[:128], values[128:]
        top_low = jnp.max(low, axis=0, keepdims=True)
        top_high = jnp.max(high, axis=0, keepdims=True)
        return jnp.concatenate(
            [
                jnp.exp(low - jnp.maximum(top_low, top_high + gap)),
                jnp.exp(high - jnp.maximum(top_low - gap, top_high)),
            ],
            axis=0,
        ).astype(BF16)

    def pair_of(step):
        return templ ^ (3 - step ^ (1 - step // 2))

    def finish(step):
        pair = pair_of(step)
        projected = dot_tn(gated[pair], w_tri)
        result = (rows_in[pair, mine, :].astype(F32) + projected).astype(BF16)
        fresh[pair] = result

        @pl.when(step == 3)
        def _():
            peers_in[templ] = result

        @pl.when(step < 3)
        def _():
            pltpu.make_async_remote_copy(
                src_ref=fresh.at[pair],
                dst_ref=peers_in.at[templ],
                send_sem=peer_send.at[step],
                recv_sem=peer_recv.at[templ],
                device_id=(pair, row, col),
                device_id_type=MESH,
            ).start()

    def attend(count, carry):
        heads, turn = count // 2, count % 2

        @pl.when(turn == 0)
        def _():
            drain(bias_in.at[heads], bias_recv.at[heads])
            first_half = iota((256, 128), 1) < 64
            one = bias_in[heads, 0].astype(F32)
            two = bias_in[heads, 1].astype(F32)
            bias_full[0] = jnp.where(first_half, one, pltpu.roll(two, 64, 1))
            bias_full[1] = jnp.where(first_half, pltpu.roll(one, 64, 1), two)

        for step in (2 * turn, 2 * turn + 1):
            pair = pair_of(step)
            for side in range(2):
                both = scores[pair, 2 * side + heads]
                weights = jnp.concatenate(
                    [soft(both[:, :128], bias_full[0]), soft(both[:, 128:], bias_full[1])], axis=1
                )
                place = pl.ds(pl.multiple_of(64 * side + 32 * heads, 32), 32)
                mixed = dot_nn(jnp.concatenate([values[pair, place, :], ones_rows], axis=0), weights)
                attended = jnp.concatenate(
                    [mixed[:16, :128] / mixed[32:, :128], mixed[16:32, 128:] / mixed[32:, 128:]], axis=0
                )
                gated[pair, place, :] = (attended * gates[pair, place, :]).astype(BF16)

        @pl.when(heads == 1)
        def _():
            finish(2 * turn)
            finish(2 * turn + 1)

        return carry

    lax.fori_loop(0, 4, attend, 0)

    new_place = new_out.at[pl.ds(4 * chunk, 4)]

    def returned(to_chunk):
        return fresh.at[:, pl.ds(pl.multiple_of(16 * to_chunk, 16), 16), :]

    def send_new(step, carry):
        to_chunk = (chunk + step) % 8
        pltpu.make_async_remote_copy(
            src_ref=returned(to_chunk),
            dst_ref=new_place,
            send_sem=new_send,
            recv_sem=new_recv,
            device_id=(templ, row, 8 * half + to_chunk),
            device_id_type=MESH,
        ).start()
        return carry

    lax.fori_loop(1, 8, send_new, 0)
    pltpu.make_async_copy(returned(chunk), new_place, new_recv).start()

    pltpu.make_async_copy(main_in, main_in, main_recv).wait()
    main_query = 0.25 * (
        dot_nt(main_in[0], jnp.concatenate([w_query, nothing], axis=0))
        + dot_nt(main_in[1], jnp.concatenate([nothing, w_query], axis=0))
    )

    def wait_peer(step, carry):
        source = (templ + step) % 4
        pltpu.make_async_copy(peers_in.at[source], peers_in.at[source], peer_recv.at[source]).wait()
        return carry

    lax.fori_loop(1, 4, wait_peer, 0)
    peers_normed = pair_norm(peers_in[...].reshape(512, 128), averager, merge_gain)
    merge_keys = dot_nn(peers_normed, w_merge_key).astype(BF16).astype(F32).reshape(4, 128, 128)
    shown = dot_nn(peers_normed, w_merge_value).astype(BF16).astype(F32).reshape(4, 128, 128)
    products = split_dot((main_query[None] * merge_keys).reshape(512, 128), summer).reshape(4, 128, 128)
    merge_scores = []
    for other in range(4):
        valid = coverage_ref[row_block, other] * coverage_ref[half, other] * mask_ref[row_block, half]
        merge_scores.append(products[other] + MASK_SHIFT * (valid.astype(F32) - 1.0))
    highest = jnp.maximum(
        jnp.maximum(merge_scores[0], merge_scores[1]), jnp.maximum(merge_scores[2], merge_scores[3])
    )
    weights = [jnp.exp(one - highest) for one in merge_scores]
    total = (weights[0] + weights[1]) + (weights[2] + weights[3])
    blend = (weights[0] * shown[0] + weights[1] * shown[1]) + (weights[2] * shown[2] + weights[3] * shown[3])
    merged[...] = (blend / total).astype(BF16)

    pltpu.make_async_copy(
        merged.at[pl.ds(pl.multiple_of(16 * chunk, 16), 16), :],
        merged_out.at[4 * chunk + templ],
        merged_recv,
    ).start()

    pl.semaphore_wait(second_sem, 3)

    def send_merged(step, carry):
        to_templ, to_chunk = templ ^ (3 - step % 4), (chunk + 3 + step // 4) % 8

        @pl.when((to_templ != templ) | (to_chunk != chunk))
        def _():
            pltpu.make_async_remote_copy(
                src_ref=merged.at[pl.ds(pl.multiple_of(16 * to_chunk, 16), 16), :],
                dst_ref=merged_out.at[4 * chunk + templ],
                send_sem=merged_send,
                recv_sem=merged_recv,
                device_id=(to_templ, row, 8 * half + to_chunk),
                device_id_type=MESH,
            ).start()

        return carry

    lax.fori_loop(0, 32, send_merged, 0)

    for step in range(3):
        drain(fresh.at[0], peer_send.at[step])
    drain(sizes.at[pl.ds(0, 30)], rows_send)
    drain(sizes.at[pl.ds(0, 3)], cross_send)
    for heads in range(2):
        drain(sizes.at[pl.ds(0, 15)], bias_send.at[heads])
    drain(sizes.at[pl.ds(0, 7)], main_send)
    drain(sizes.at[pl.ds(0, 14)], new_send)
    drain(packed.at[pl.ds(0, 31)], merged_send)
    drain(new_out, new_recv)
    drain(merged_out, merged_recv)


def out_kernel(new_ref, merged_ref, w_out_ref, templ_ref, embedding_ref):
    new = new_ref[...]
    templ_ref[0, pl.ds(0, 32)] = new[:, :, :64]
    templ_ref[0, pl.ds(32, 32)] = new[:, :, 64:]
    merged = merged_ref[...].reshape(512, 128)
    w_out = w_out_ref[...]
    nothing = jnp.zeros_like(w_out)
    first = dot_nn(merged, jnp.concatenate([w_out, nothing], axis=0))
    second = dot_nn(merged, jnp.concatenate([nothing, w_out], axis=0))
    embedding_ref[pl.ds(0, 32)] = first.astype(BF16).reshape(32, 16, 128)
    embedding_ref[pl.ds(32, 32)] = second.astype(BF16).reshape(32, 16, 128)


def on_device(
    templ_pair,
    main_pair,
    coverage,
    pair_mask,
    tri_gain,
    w_project,
    w_bias,
    w_tri_out,
    merge_gain,
    w_merge_q,
    w_merge_kv,
    w_merge_out,
):
    vmem = pl.BlockSpec(memory_space=pltpu.VMEM)
    anywhere = pl.BlockSpec(memory_space=pl.ANY)
    piece = jax.ShapeDtypeStruct((32, 16, 128), BF16)
    dma = pltpu.SemaphoreType.DMA
    new, merged = pl.pallas_call(
        pair_kernel,
        out_shape=(piece, piece),
        in_specs=[pl.BlockSpec(memory_space=pltpu.HBM)] * 11,
        out_specs=(anywhere, anywhere),
        scratch_shapes=[
            pltpu.VMEM((64, 16, 64), BF16),
            pltpu.SMEM((2, 4), jnp.int32),
            pltpu.SMEM((2, 2), jnp.int32),
            pltpu.VMEM((1, 64), F32),
            pltpu.VMEM((64, 256), BF16),
            pltpu.VMEM((4, 64), BF16),
            pltpu.VMEM((64, 64), BF16),
            pltpu.VMEM((1, 64), F32),
            pltpu.VMEM((64, 128), BF16),
            pltpu.VMEM((64, 128), BF16),
            pltpu.VMEM((32, 16, 128), BF16),
            pltpu.VMEM((4, 256, 128), BF16),
            pltpu.VMEM((2, 4, 16, 128), BF16),
            pltpu.VMEM((2, 2, 256, 128), BF16),
            pltpu.VMEM((2, 256, 128), F32),
            pltpu.VMEM((2, 128, 128), BF16),
            pltpu.VMEM((4, 256, 128), BF16),
            pltpu.VMEM((4, 256, 128), BF16),
            pltpu.VMEM((4, 128, 256), BF16),
            pltpu.VMEM((4, 128, 128), BF16),
            pltpu.VMEM((4, 128, 128), F32),
            pltpu.VMEM((4, 4, 256, 256), F32),
            pltpu.VMEM((4, 128, 128), BF16),
            pltpu.VMEM((4, 128, 128), BF16),
            pltpu.VMEM((4, 128, 128), BF16),
            pltpu.VMEM((128, 128), BF16),
            pltpu.VMEM((32, 16, 256), BF16),
            dma((10,)),
            dma,
            dma,
            dma,
            dma,
            dma((2,)),
            dma((2,)),
            dma,
            dma,
            dma((4,)),
            dma((4,)),
            dma,
            dma,
            dma,
            dma,
            pltpu.SemaphoreType.REGULAR,
        ],
        compiler_params=pltpu.CompilerParams(
            collective_id=0, has_side_effects=True, vmem_limit_bytes=64 * 1024 * 1024
        ),
        name="pair_kernel",
    )(
        templ_pair[0],
        main_pair.reshape(2, 32, 16, 128),
        coverage.T,
        pair_mask,
        tri_gain.reshape(1, 64),
        w_project,
        w_bias.T,
        w_tri_out,
        merge_gain.reshape(1, 64),
        w_merge_q.T,
        w_merge_kv,
    )
    return pl.pallas_call(
        out_kernel,
        out_shape=(
            jax.ShapeDtypeStruct((1, 64, 16, 64), BF16),
            jax.ShapeDtypeStruct((64, 16, 128), BF16),
        ),
        in_specs=[vmem] * 3,
        out_specs=(vmem, vmem),
        compiler_params=pltpu.CompilerParams(vmem_limit_bytes=64 * 1024 * 1024),
        name="out_kernel",
    )(new, merged, w_merge_out)


def solution(mesh):
    whole = P()
    tiles = P("tmpl", "row", "col", None)
    pairs = P("row", "col", None)
    return jax.shard_map(
        on_device,
        mesh=mesh,
        in_specs=(tiles, pairs) + (whole,) * 10,
        out_specs=(tiles, pairs),
        check_vma=False,
    )
```

```python
import jax
import jax.numpy as jnp
from jax import lax
from jax.experimental import pallas as pl
from jax.experimental.pallas import tpu as pltpu
from jax.sharding import PartitionSpec as P

MASK_SHIFT = 10000.0
EPSILON = 1e-05
MESH = pl.DeviceIdType.MESH
F32 = jnp.float32
BF16 = jnp.bfloat16


def iota(shape, axis):
    return lax.broadcasted_iota(jnp.int32, shape, axis)


def dot_nn(a, b):
    return lax.dot_general(a, b, (((1,), (0,)), ((), ())), preferred_element_type=F32)


def dot_nt(a, b):
    return lax.dot_general(a, b, (((1,), (1,)), ((), ())), preferred_element_type=F32)


def dot_tn(a, b):
    return lax.dot_general(a, b, (((0,), (0,)), ((), ())), preferred_element_type=F32)


def split_dot(values, weights):
    high = values.astype(BF16)
    low = (values - high.astype(F32)).astype(BF16)
    return dot_nn(high, weights) + dot_nn(low, weights)


def pair_norm(values, averager, gain):
    center = values.astype(F32) - dot_nn(values, averager)
    spread = split_dot(center * center, averager)
    return (center * lax.rsqrt(spread + EPSILON) * gain).astype(BF16)


def ones_where(condition):
    return jnp.where(condition, 1.0, 0.0).astype(BF16)


def diagonal(doubled):
    both = jnp.concatenate([doubled, doubled], axis=0)
    keep = (iota((128, 128), 0) < 64) == (iota((128, 128), 1) < 64)
    return jnp.where(keep, both, 0.0).astype(BF16)


def pick_columns(width, first):
    return ones_where(iota((width, 128), 0) == first + iota((width, 128), 1) % 64)


def pair_kernel(
    templ_hbm,
    main_hbm,
    coverage_hbm,
    mask_hbm,
    tri_gain_hbm,
    w_project_hbm,
    w_bias_hbm,
    w_tri_hbm,
    merge_gain_hbm,
    w_query_hbm,
    w_kv_hbm,
    new_out,
    merged_out,
    tile,
    coverage_ref,
    mask_ref,
    tri_gain_ref,
    w_project_ref,
    w_bias_ref,
    w_tri_ref,
    merge_gain_ref,
    w_query_ref,
    w_kv_ref,
    packed,
    rows_in,
    bias_rows,
    bias_in,
    bias_full,
    main_in,
    normed,
    keys,
    values,
    queries,
    gates,
    scores,
    gated,
    fresh,
    peers_in,
    merged,
    sizes,
    load_sem,
    rows_send,
    rows_recv,
    cross_send,
    cross_recv,
    bias_send,
    bias_recv,
    main_send,
    main_recv,
    peer_send,
    peer_recv,
    new_send,
    new_recv,
    merged_send,
    merged_recv,
    second_sem,
):
    templ = lax.axis_index("tmpl")
    row = lax.axis_index("row")
    col = lax.axis_index("col")
    plane = col // 2
    half, chunk = col // 8, col % 8
    own_cols = pl.ds(pl.multiple_of(16 * col, 16), 16)

    loads = [
        pltpu.make_async_copy(source, target, load_sem.at[index])
        for index, (source, target) in enumerate(
            (
                (templ_hbm, tile),
                (tri_gain_hbm, tri_gain_ref),
                (w_bias_hbm, w_bias_ref),
                (w_project_hbm, w_project_ref),
                (w_tri_hbm, w_tri_ref),
                (merge_gain_hbm, merge_gain_ref),
                (w_query_hbm, w_query_ref),
                (w_kv_hbm, w_kv_ref),
                (coverage_hbm, coverage_ref),
                (mask_hbm, mask_ref),
            )
        )
    ]
    barrier = pltpu.get_barrier_semaphore()
    for step in range(1, 16):
        pl.semaphore_signal(barrier, inc=1, device_id=(templ, row, (col + step) % 16), device_id_type=MESH)
    for step in range(1, 4):
        pl.semaphore_signal(barrier, inc=1, device_id=(templ, (row + step) % 4, col), device_id_type=MESH)
        pl.semaphore_signal(barrier, inc=1, device_id=((templ + step) % 4, row, col), device_id_type=MESH)
    for load in loads:
        load.start()

    for load in loads[:3]:
        load.wait()
    eye = iota((64, 128), 0)
    lane = iota((64, 128), 1)
    low_rows = tile[pl.ds(0, 32)].reshape(512, 64)
    high_rows = tile[pl.ds(32, 32)].reshape(512, 64)
    together = dot_nn(low_rows, ones_where(eye == lane)) + dot_nn(high_rows, ones_where(eye + 64 == lane))
    packed[...] = together.astype(BF16).reshape(32, 16, 128)

    averager = jnp.where(
        (iota((128, 128), 0) < 64) == (iota((128, 128), 1) < 64), 1.0 / 64, 0.0
    ).astype(BF16)
    tri_gain = jnp.concatenate([tri_gain_ref[...], tri_gain_ref[...]], axis=1)

    own_normed = pair_norm(packed[...].reshape(512, 128), averager, tri_gain)
    w_bias = dot_nn(w_bias_ref[...], pick_columns(64, 0))
    which = iota((256, 128), 0)
    spread_bias = jnp.zeros((256, 128), F32)
    for head in range(4):
        spread_bias = jnp.where(which // 64 == head, w_bias[head : head + 1, :], spread_bias)
    spread_bias = jnp.where((which // 32) % 2 == iota((256, 128), 1) // 64, spread_bias, 0.0).astype(BF16)
    every_bias = dot_nt(own_normed, spread_bias).reshape(32, 16, 256)
    place = iota((16, 256), 1) % 32
    chosen = jnp.zeros((16, 256), F32)
    for index in range(32):
        chosen = jnp.where(place == index, every_bias[index], chosen)
    chosen = chosen.astype(BF16)
    bias_rows[0, row] = chosen[:, :128]
    bias_rows[1, row] = chosen[:, 128:]

    pl.semaphore_wait(barrier, 21)
    for step in range(1, 4):
        pl.semaphore_signal(second_sem, inc=1, device_id=((templ + step) % 4, row, col), device_id_type=MESH)

    def far_first(index):
        away = (index // 2 + 1) // 2 * (2 * (index // 2 % 2) - 1)
        return 2 * ((plane + 4 + away) % 8) + (col + index) % 2

    def send_to_columns(source_of, target, local_target, send_sem, recv_sem):
        def one(index, carry):
            to = far_first(index)
            pltpu.make_async_remote_copy(
                src_ref=source_of(to),
                dst_ref=target,
                send_sem=send_sem,
                recv_sem=recv_sem,
                device_id=(templ, row, to),
                device_id_type=MESH,
            ).start()
            return carry

        lax.fori_loop(0, 14, one, 0)
        one(15, 0)
        pltpu.make_async_copy(source_of(col), local_target, recv_sem).start()

    rows_place = rows_in.at[:, own_cols, :]
    send_to_columns(
        lambda to: packed.at[pl.ds(4 * (to % 8), 4)], rows_place, rows_place, rows_send, rows_recv
    )

    for step in range(1, 4):
        pltpu.make_async_remote_copy(
            src_ref=bias_rows.at[:, row],
            dst_ref=bias_rows.at[:, row],
            send_sem=cross_send,
            recv_sem=cross_recv,
            device_id=(templ, (row + step) % 4, col),
            device_id_type=MESH,
        ).start()

    for load in loads[3:]:
        load.wait()
    w_project = w_project_ref[...]
    double = pick_columns(64, 0)

    def turned(first):
        columns = ones_where(iota((128, 256), 1) == first + iota((128, 256), 0) % 64)
        wide = dot_nn(dot_nt(columns, w_project).astype(BF16), double)
        keep = (iota((128, 128), 0) < 64) == (iota((128, 128), 1) < 64)
        return jnp.where(keep, wide, 0.0).astype(BF16)

    turned_query, turned_value, turned_gate = turned(0), turned(128), turned(192)
    w_key = diagonal(dot_nn(w_project, pick_columns(256, 64)))
    w_tri = diagonal(dot_nn(w_tri_ref[...], double))
    ones_rows = jnp.ones((16, 256), BF16)
    head_of = iota((128, 128), 0) // 16

    w_query = w_query_ref[...]
    nothing = jnp.zeros_like(w_query)
    w_kv = w_kv_ref[...]
    w_merge_key = diagonal(dot_nn(w_kv, pick_columns(128, 0)))
    w_merge_value = diagonal(dot_nn(w_kv, pick_columns(128, 64)))
    merge_gain = jnp.concatenate([merge_gain_ref[...], merge_gain_ref[...]], axis=1)
    summer = ones_where(iota((128, 128), 0) // 16 == iota((128, 128), 1) // 16)

    def drain(ref, sem):
        pltpu.make_async_copy(ref, ref, sem).wait()

    drain(sizes.at[pl.ds(0, 3)], cross_recv)
    for heads in range(2):
        bias_place = bias_in.at[heads, :, own_cols, :]
        send_to_columns(
            lambda to, heads=heads: bias_rows.at[heads, pl.ds(2 * (to // 8), 2)],
            bias_place,
            bias_place,
            bias_send.at[heads],
            bias_recv.at[heads],
        )

    main_place = main_in.at[:, pl.ds(pl.multiple_of(16 * chunk, 16), 16), :]
    pltpu.make_async_copy(main_hbm.at[:, 4 * chunk + templ], main_place, main_recv).start()

    def send_main(step, carry):
        to_chunk = (chunk + step) % 8
        pltpu.make_async_remote_copy(
            src_ref=main_hbm.at[:, 4 * to_chunk + templ],
            dst_ref=main_place,
            send_sem=main_send,
            recv_sem=main_recv,
            device_id=(templ, row, 8 * half + to_chunk),
            device_id_type=MESH,
        ).start()
        return carry

    lax.fori_loop(1, 8, send_main, 0)

    row_block = row // 2
    cover_row = coverage_ref[row_block, templ]
    shift_low = MASK_SHIFT * ((cover_row * coverage_ref[0, templ] * mask_ref[row_block, 0]).astype(F32) - 1.0)
    shift_high = MASK_SHIFT * ((cover_row * coverage_ref[1, templ] * mask_ref[row_block, 1]).astype(F32) - 1.0)
    gap = shift_high - shift_low
    mine = pl.ds(pl.multiple_of(128 * half, 128), 128)

    drain(rows_in, rows_recv)
    every_normed = pair_norm(rows_in[...].reshape(1024, 128), averager, tri_gain)
    normed[...] = every_normed.reshape(4, 256, 128)
    keys[...] = dot_nn(every_normed, w_key).astype(BF16).reshape(4, 256, 128)
    every_value = dot_nt(turned_value, every_normed).astype(BF16)
    own_part = normed[:, mine, :].reshape(512, 128)
    every_query = (dot_nt(turned_query, own_part) * 0.25).astype(BF16)
    every_gate = jax.nn.sigmoid(dot_nt(turned_gate, own_part))
    for pair in range(4):
        values[pair] = every_value[:, 256 * pair : 256 * pair + 256]
        queries[pair] = every_query[:, 128 * pair : 128 * pair + 128]
        gates[pair] = every_gate[:, 128 * pair : 128 * pair + 128]

    def score(pair, carry):
        pair_keys, pair_queries = keys[pair], queries[pair]
        nothing = jnp.zeros_like(pair_queries)
        for index in range(4):
            two_heads = jnp.concatenate(
                [
                    jnp.where(head_of == 2 * index, pair_queries, nothing),
                    jnp.where(head_of == 2 * index + 1, pair_queries, nothing),
                ],
                axis=1,
            )
            scores[pair, index] = dot_nn(pair_keys, two_heads)
        return carry

    lax.fori_loop(0, 4, score, 0)

    def soft(values, bias):
        values = values + bias
        low, high = values[:128], values[128:]
        top_low = jnp.max(low, axis=0, keepdims=True)
        top_high = jnp.max(high, axis=0, keepdims=True)
        return jnp.concatenate(
            [
                jnp.exp(low - jnp.maximum(top_low, top_high + gap)),
                jnp.exp(high - jnp.maximum(top_low - gap, top_high)),
            ],
            axis=0,
        ).astype(BF16)

    def pair_of(step):
        return templ ^ (3 - step ^ (1 - step // 2))

    def finish(step):
        pair = pair_of(step)
        projected = dot_tn(gated[pair], w_tri)
        result = (rows_in[pair, mine, :].astype(F32) + projected).astype(BF16)
        fresh[pair] = result

        @pl.when(step == 3)
        def _():
            peers_in[templ] = result

        @pl.when(step < 3)
        def _():
            pltpu.make_async_remote_copy(
                src_ref=fresh.at[pair],
                dst_ref=peers_in.at[templ],
                send_sem=peer_send.at[step],
                recv_sem=peer_recv.at[templ],
                device_id=(pair, row, col),
                device_id_type=MESH,
            ).start()

    def attend(count, carry):
        heads, turn = count // 2, count % 2

        @pl.when(turn == 0)
        def _():
            drain(bias_in.at[heads], bias_recv.at[heads])
            first_half = iota((256, 128), 1) < 64
            one = bias_in[heads, 0].astype(F32)
            two = bias_in[heads, 1].astype(F32)
            bias_full[0] = jnp.where(first_half, one, pltpu.roll(two, 64, 1))
            bias_full[1] = jnp.where(first_half, pltpu.roll(one, 64, 1), two)

        for step in (2 * turn, 2 * turn + 1):
            pair = pair_of(step)
            for side in range(2):
                both = scores[pair, 2 * side + heads]
                weights = jnp.concatenate(
                    [soft(both[:, :128], bias_full[0]), soft(both[:, 128:], bias_full[1])], axis=1
                )
                place = pl.ds(pl.multiple_of(64 * side + 32 * heads, 32), 32)
                mixed = dot_nn(jnp.concatenate([values[pair, place, :], ones_rows], axis=0), weights)
                attended = jnp.concatenate(
                    [mixed[:16, :128] / mixed[32:, :128], mixed[16:32, 128:] / mixed[32:, 128:]], axis=0
                )
                gated[pair, place, :] = (attended * gates[pair, place, :]).astype(BF16)

            @pl.when(heads == 1)
            def _(step=step):
                finish(step)

        return carry

    lax.fori_loop(0, 4, attend, 0)

    new_place = new_out.at[pl.ds(4 * chunk, 4)]

    def returned(to_chunk):
        return fresh.at[:, pl.ds(pl.multiple_of(16 * to_chunk, 16), 16), :]

    def send_new(step, carry):
        to_chunk = (chunk + step) % 8
        pltpu.make_async_remote_copy(
            src_ref=returned(to_chunk),
            dst_ref=new_place,
            send_sem=new_send,
            recv_sem=new_recv,
            device_id=(templ, row, 8 * half + to_chunk),
            device_id_type=MESH,
        ).start()
        return carry

    lax.fori_loop(1, 8, send_new, 0)
    pltpu.make_async_copy(returned(chunk), new_place, new_recv).start()

    pltpu.make_async_copy(main_in, main_in, main_recv).wait()
    main_query = 0.25 * (
        dot_nt(main_in[0], jnp.concatenate([w_query, nothing], axis=0))
        + dot_nt(main_in[1], jnp.concatenate([nothing, w_query], axis=0))
    )

    def wait_peer(step, carry):
        source = (templ + step) % 4
        pltpu.make_async_copy(peers_in.at[source], peers_in.at[source], peer_recv.at[source]).wait()
        return carry

    lax.fori_loop(1, 4, wait_peer, 0)
    peers_normed = pair_norm(peers_in[...].reshape(512, 128), averager, merge_gain)
    merge_keys = dot_nn(peers_normed, w_merge_key).astype(BF16).astype(F32).reshape(4, 128, 128)
    shown = dot_nn(peers_normed, w_merge_value).astype(BF16).astype(F32).reshape(4, 128, 128)
    products = split_dot((main_query[None] * merge_keys).reshape(512, 128), summer).reshape(4, 128, 128)
    merge_scores = []
    for other in range(4):
        valid = coverage_ref[row_block, other] * coverage_ref[half, other] * mask_ref[row_block, half]
        merge_scores.append(products[other] + MASK_SHIFT * (valid.astype(F32) - 1.0))
    highest = jnp.maximum(
        jnp.maximum(merge_scores[0], merge_scores[1]), jnp.maximum(merge_scores[2], merge_scores[3])
    )
    weights = [jnp.exp(one - highest) for one in merge_scores]
    total = (weights[0] + weights[1]) + (weights[2] + weights[3])
    blend = (weights[0] * shown[0] + weights[1] * shown[1]) + (weights[2] * shown[2] + weights[3] * shown[3])
    merged[...] = (blend / total).astype(BF16)

    pltpu.make_async_copy(
        merged.at[pl.ds(pl.multiple_of(16 * chunk, 16), 16), :],
        merged_out.at[4 * chunk + templ],
        merged_recv,
    ).start()

    pl.semaphore_wait(second_sem, 3)

    def send_merged(step, carry):
        to_templ, to_chunk = templ ^ (3 - step % 4), (chunk + 3 + step // 4) % 8

        @pl.when((to_templ != templ) | (to_chunk != chunk))
        def _():
            pltpu.make_async_remote_copy(
                src_ref=merged.at[pl.ds(pl.multiple_of(16 * to_chunk, 16), 16), :],
                dst_ref=merged_out.at[4 * chunk + templ],
                send_sem=merged_send,
                recv_sem=merged_recv,
                device_id=(to_templ, row, 8 * half + to_chunk),
                device_id_type=MESH,
            ).start()

        return carry

    lax.fori_loop(0, 32, send_merged, 0)

    for step in range(3):
        drain(fresh.at[0], peer_send.at[step])
    drain(sizes.at[pl.ds(0, 30)], rows_send)
    drain(sizes.at[pl.ds(0, 3)], cross_send)
    for heads in range(2):
        drain(sizes.at[pl.ds(0, 15)], bias_send.at[heads])
    drain(sizes.at[pl.ds(0, 7)], main_send)
    drain(sizes.at[pl.ds(0, 14)], new_send)
    drain(packed.at[pl.ds(0, 31)], merged_send)
    drain(new_out, new_recv)
    drain(merged_out, merged_recv)


def out_kernel(new_ref, merged_ref, w_out_ref, templ_ref, embedding_ref):
    new = new_ref[...]
    templ_ref[0, pl.ds(0, 32)] = new[:, :, :64]
    templ_ref[0, pl.ds(32, 32)] = new[:, :, 64:]
    merged = merged_ref[...].reshape(512, 128)
    w_out = w_out_ref[...]
    nothing = jnp.zeros_like(w_out)
    first = dot_nn(merged, jnp.concatenate([w_out, nothing], axis=0))
    second = dot_nn(merged, jnp.concatenate([nothing, w_out], axis=0))
    embedding_ref[pl.ds(0, 32)] = first.astype(BF16).reshape(32, 16, 128)
    embedding_ref[pl.ds(32, 32)] = second.astype(BF16).reshape(32, 16, 128)


def on_device(
    templ_pair,
    main_pair,
    coverage,
    pair_mask,
    tri_gain,
    w_project,
    w_bias,
    w_tri_out,
    merge_gain,
    w_merge_q,
    w_merge_kv,
    w_merge_out,
):
    vmem = pl.BlockSpec(memory_space=pltpu.VMEM)
    anywhere = pl.BlockSpec(memory_space=pl.ANY)
    piece = jax.ShapeDtypeStruct((32, 16, 128), BF16)
    dma = pltpu.SemaphoreType.DMA
    new, merged = pl.pallas_call(
        pair_kernel,
        out_shape=(piece, piece),
        in_specs=[pl.BlockSpec(memory_space=pltpu.HBM)] * 11,
        out_specs=(anywhere, anywhere),
        scratch_shapes=[
            pltpu.VMEM((64, 16, 64), BF16),
            pltpu.SMEM((2, 4), jnp.int32),
            pltpu.SMEM((2, 2), jnp.int32),
            pltpu.VMEM((1, 64), F32),
            pltpu.VMEM((64, 256), BF16),
            pltpu.VMEM((4, 64), BF16),
            pltpu.VMEM((64, 64), BF16),
            pltpu.VMEM((1, 64), F32),
            pltpu.VMEM((64, 128), BF16),
            pltpu.VMEM((64, 128), BF16),
            pltpu.VMEM((32, 16, 128), BF16),
            pltpu.VMEM((4, 256, 128), BF16),
            pltpu.VMEM((2, 4, 16, 128), BF16),
            pltpu.VMEM((2, 2, 256, 128), BF16),
            pltpu.VMEM((2, 256, 128), F32),
            pltpu.VMEM((2, 128, 128), BF16),
            pltpu.VMEM((4, 256, 128), BF16),
            pltpu.VMEM((4, 256, 128), BF16),
            pltpu.VMEM((4, 128, 256), BF16),
            pltpu.VMEM((4, 128, 128), BF16),
            pltpu.VMEM((4, 128, 128), F32),
            pltpu.VMEM((4, 4, 256, 256), F32),
            pltpu.VMEM((4, 128, 128), BF16),
            pltpu.VMEM((4, 128, 128), BF16),
            pltpu.VMEM((4, 128, 128), BF16),
            pltpu.VMEM((128, 128), BF16),
            pltpu.VMEM((32, 16, 256), BF16),
            dma((10,)),
            dma,
            dma,
            dma,
            dma,
            dma((2,)),
            dma((2,)),
            dma,
            dma,
            dma((4,)),
            dma((4,)),
            dma,
            dma,
            dma,
            dma,
            pltpu.SemaphoreType.REGULAR,
        ],
        compiler_params=pltpu.CompilerParams(
            collective_id=0, has_side_effects=True, vmem_limit_bytes=64 * 1024 * 1024
        ),
        name="pair_kernel",
    )(
        templ_pair[0],
        main_pair.reshape(2, 32, 16, 128),
        coverage.T,
        pair_mask,
        tri_gain.reshape(1, 64),
        w_project,
        w_bias.T,
        w_tri_out,
        merge_gain.reshape(1, 64),
        w_merge_q.T,
        w_merge_kv,
    )
    return pl.pallas_call(
        out_kernel,
        out_shape=(
            jax.ShapeDtypeStruct((1, 64, 16, 64), BF16),
            jax.ShapeDtypeStruct((64, 16, 128), BF16),
        ),
        in_specs=[vmem] * 3,
        out_specs=(vmem, vmem),
        compiler_params=pltpu.CompilerParams(vmem_limit_bytes=64 * 1024 * 1024),
        name="out_kernel",
    )(new, merged, w_merge_out)


def solution(mesh):
    whole = P()
    tiles = P("tmpl", "row", "col", None)
    pairs = P("row", "col", None)
    return jax.shard_map(
        on_device,
        mesh=mesh,
        in_specs=(tiles, pairs) + (whole,) * 10,
        out_specs=(tiles, pairs),
        check_vma=False,
    )
```

```python
import jax
import jax.numpy as jnp
from jax import lax
from jax.experimental import pallas as pl
from jax.experimental.pallas import tpu as pltpu
from jax.sharding import PartitionSpec as P

MASK_SHIFT = 10000.0
EPSILON = 1e-05
MESH = pl.DeviceIdType.MESH
F32 = jnp.float32
BF16 = jnp.bfloat16


def iota(shape, axis):
    return lax.broadcasted_iota(jnp.int32, shape, axis)


def dot_nn(a, b):
    return lax.dot_general(a, b, (((1,), (0,)), ((), ())), preferred_element_type=F32)


def dot_nt(a, b):
    return lax.dot_general(a, b, (((1,), (1,)), ((), ())), preferred_element_type=F32)


def dot_tn(a, b):
    return lax.dot_general(a, b, (((0,), (0,)), ((), ())), preferred_element_type=F32)


def split_dot(values, weights):
    high = values.astype(BF16)
    low = (values - high.astype(F32)).astype(BF16)
    return dot_nn(high, weights) + dot_nn(low, weights)


def pair_norm(values, averager, gain):
    center = values.astype(F32) - dot_nn(values, averager)
    spread = split_dot(center * center, averager)
    return (center * lax.rsqrt(spread + EPSILON) * gain).astype(BF16)


def ones_where(condition):
    return jnp.where(condition, 1.0, 0.0).astype(BF16)


def diagonal(doubled):
    both = jnp.concatenate([doubled, doubled], axis=0)
    keep = (iota((128, 128), 0) < 64) == (iota((128, 128), 1) < 64)
    return jnp.where(keep, both, 0.0).astype(BF16)


def pick_columns(width, first):
    return ones_where(iota((width, 128), 0) == first + iota((width, 128), 1) % 64)


def pair_kernel(
    templ_hbm,
    main_hbm,
    coverage_hbm,
    mask_hbm,
    tri_gain_hbm,
    w_project_hbm,
    w_bias_hbm,
    w_tri_hbm,
    merge_gain_hbm,
    w_query_hbm,
    w_kv_hbm,
    new_out,
    merged_out,
    tile,
    coverage_ref,
    mask_ref,
    tri_gain_ref,
    w_project_ref,
    w_bias_ref,
    w_tri_ref,
    merge_gain_ref,
    w_query_ref,
    w_kv_ref,
    packed,
    rows_in,
    bias_rows,
    bias_in,
    bias_full,
    main_in,
    normed,
    keys,
    values,
    queries,
    gates,
    scores,
    gated,
    fresh,
    peers_in,
    merged,
    sizes,
    load_sem,
    rows_send,
    rows_recv,
    cross_send,
    cross_recv,
    bias_send,
    bias_recv,
    main_send,
    main_recv,
    peer_send,
    peer_recv,
    new_send,
    new_recv,
    merged_send,
    merged_recv,
    second_sem,
):
    templ = lax.axis_index("tmpl")
    row = lax.axis_index("row")
    col = lax.axis_index("col")
    plane = col // 2
    half, chunk = col // 8, col % 8
    own_cols = pl.ds(pl.multiple_of(16 * col, 16), 16)

    loads = [
        pltpu.make_async_copy(source, target, load_sem.at[index])
        for index, (source, target) in enumerate(
            (
                (templ_hbm, tile),
                (tri_gain_hbm, tri_gain_ref),
                (w_bias_hbm, w_bias_ref),
                (w_project_hbm, w_project_ref),
                (w_tri_hbm, w_tri_ref),
                (merge_gain_hbm, merge_gain_ref),
                (w_query_hbm, w_query_ref),
                (w_kv_hbm, w_kv_ref),
                (coverage_hbm, coverage_ref),
                (mask_hbm, mask_ref),
            )
        )
    ]
    barrier = pltpu.get_barrier_semaphore()
    for step in range(1, 16):
        pl.semaphore_signal(barrier, inc=1, device_id=(templ, row, (col + step) % 16), device_id_type=MESH)
    for step in range(1, 4):
        pl.semaphore_signal(barrier, inc=1, device_id=(templ, (row + step) % 4, col), device_id_type=MESH)
        pl.semaphore_signal(barrier, inc=1, device_id=((templ + step) % 4, row, col), device_id_type=MESH)
    for load in loads:
        load.start()

    for load in loads[:3]:
        load.wait()
    eye = iota((64, 128), 0)
    lane = iota((64, 128), 1)
    low_rows = tile[pl.ds(0, 32)].reshape(512, 64)
    high_rows = tile[pl.ds(32, 32)].reshape(512, 64)
    together = dot_nn(low_rows, ones_where(eye == lane)) + dot_nn(high_rows, ones_where(eye + 64 == lane))
    packed[...] = together.astype(BF16).reshape(32, 16, 128)

    averager = jnp.where(
        (iota((128, 128), 0) < 64) == (iota((128, 128), 1) < 64), 1.0 / 64, 0.0
    ).astype(BF16)
    tri_gain = jnp.concatenate([tri_gain_ref[...], tri_gain_ref[...]], axis=1)

    own_normed = pair_norm(packed[...].reshape(512, 128), averager, tri_gain)
    w_bias = dot_nn(w_bias_ref[...], pick_columns(64, 0))
    which = iota((256, 128), 0)
    spread_bias = jnp.zeros((256, 128), F32)
    for head in range(4):
        spread_bias = jnp.where(which // 64 == head, w_bias[head : head + 1, :], spread_bias)
    spread_bias = jnp.where((which // 32) % 2 == iota((256, 128), 1) // 64, spread_bias, 0.0).astype(BF16)
    every_bias = dot_nt(own_normed, spread_bias).reshape(32, 16, 256)
    place = iota((16, 256), 1) % 32
    chosen = jnp.zeros((16, 256), F32)
    for index in range(32):
        chosen = jnp.where(place == index, every_bias[index], chosen)
    chosen = chosen.astype(BF16)
    bias_rows[0, row] = chosen[:, :128]
    bias_rows[1, row] = chosen[:, 128:]

    pl.semaphore_wait(barrier, 21)
    for step in range(1, 4):
        pl.semaphore_signal(second_sem, inc=1, device_id=((templ + step) % 4, row, col), device_id_type=MESH)

    def far_first(index):
        away = (index // 2 + 1) // 2 * (2 * (index // 2 % 2) - 1)
        return 2 * ((plane + 4 + away) % 8) + (col + index) % 2

    def send_to_columns(source_of, target, local_target, send_sem, recv_sem):
        def one(index, carry):
            to = far_first(index)
            pltpu.make_async_remote_copy(
                src_ref=source_of(to),
                dst_ref=target,
                send_sem=send_sem,
                recv_sem=recv_sem,
                device_id=(templ, row, to),
                device_id_type=MESH,
            ).start()
            return carry

        lax.fori_loop(0, 14, one, 0)
        one(15, 0)
        pltpu.make_async_copy(source_of(col), local_target, recv_sem).start()

    rows_place = rows_in.at[:, own_cols, :]
    send_to_columns(
        lambda to: packed.at[pl.ds(4 * (to % 8), 4)], rows_place, rows_place, rows_send, rows_recv
    )

    for step in range(1, 4):
        pltpu.make_async_remote_copy(
            src_ref=bias_rows.at[:, row],
            dst_ref=bias_rows.at[:, row],
            send_sem=cross_send,
            recv_sem=cross_recv,
            device_id=(templ, (row + step) % 4, col),
            device_id_type=MESH,
        ).start()

    for load in loads[3:]:
        load.wait()
    w_project = w_project_ref[...]
    double = pick_columns(64, 0)

    def turned(first):
        columns = ones_where(iota((128, 256), 1) == first + iota((128, 256), 0) % 64)
        wide = dot_nn(dot_nt(columns, w_project).astype(BF16), double)
        keep = (iota((128, 128), 0) < 64) == (iota((128, 128), 1) < 64)
        return jnp.where(keep, wide, 0.0).astype(BF16)

    turned_query, turned_value, turned_gate = turned(0), turned(128), turned(192)
    w_key = diagonal(dot_nn(w_project, pick_columns(256, 64)))
    w_tri = diagonal(dot_nn(w_tri_ref[...], double))
    ones_rows = jnp.ones((16, 256), BF16)
    head_of = iota((128, 128), 0) // 16

    w_query = w_query_ref[...]
    nothing = jnp.zeros_like(w_query)
    w_kv = w_kv_ref[...]
    w_merge_key = diagonal(dot_nn(w_kv, pick_columns(128, 0)))
    w_merge_value = diagonal(dot_nn(w_kv, pick_columns(128, 64)))
    merge_gain = jnp.concatenate([merge_gain_ref[...], merge_gain_ref[...]], axis=1)
    summer = ones_where(iota((128, 128), 0) // 16 == iota((128, 128), 1) // 16)

    def drain(ref, sem):
        pltpu.make_async_copy(ref, ref, sem).wait()

    drain(sizes.at[pl.ds(0, 3)], cross_recv)
    for heads in range(2):
        bias_place = bias_in.at[heads, :, own_cols, :]
        send_to_columns(
            lambda to, heads=heads: bias_rows.at[heads, pl.ds(2 * (to // 8), 2)],
            bias_place,
            bias_place,
            bias_send.at[heads],
            bias_recv.at[heads],
        )

    main_place = main_in.at[:, pl.ds(pl.multiple_of(16 * chunk, 16), 16), :]
    pltpu.make_async_copy(main_hbm.at[:, 4 * chunk + templ], main_place, main_recv).start()

    def send_main(step, carry):
        to_chunk = (chunk + step) % 8
        pltpu.make_async_remote_copy(
            src_ref=main_hbm.at[:, 4 * to_chunk + templ],
            dst_ref=main_place,
            send_sem=main_send,
            recv_sem=main_recv,
            device_id=(templ, row, 8 * half + to_chunk),
            device_id_type=MESH,
        ).start()
        return carry

    lax.fori_loop(1, 8, send_main, 0)

    row_block = row // 2
    cover_row = coverage_ref[row_block, templ]
    shift_low = MASK_SHIFT * ((cover_row * coverage_ref[0, templ] * mask_ref[row_block, 0]).astype(F32) - 1.0)
    shift_high = MASK_SHIFT * ((cover_row * coverage_ref[1, templ] * mask_ref[row_block, 1]).astype(F32) - 1.0)
    gap = shift_high - shift_low
    mine = pl.ds(pl.multiple_of(128 * half, 128), 128)

    drain(rows_in, rows_recv)
    every_normed = pair_norm(rows_in[...].reshape(1024, 128), averager, tri_gain)
    normed[...] = every_normed.reshape(4, 256, 128)
    keys[...] = dot_nn(every_normed, w_key).astype(BF16).reshape(4, 256, 128)
    every_value = dot_nt(turned_value, every_normed).astype(BF16)
    own_part = normed[:, mine, :].reshape(512, 128)
    every_query = (dot_nt(turned_query, own_part) * 0.25).astype(BF16)
    every_gate = jax.nn.sigmoid(dot_nt(turned_gate, own_part))
    for pair in range(4):
        values[pair] = every_value[:, 256 * pair : 256 * pair + 256]
        queries[pair] = every_query[:, 128 * pair : 128 * pair + 128]
        gates[pair] = every_gate[:, 128 * pair : 128 * pair + 128]

    def score(pair, carry):
        pair_keys, pair_queries = keys[pair], queries[pair]
        nothing = jnp.zeros_like(pair_queries)
        for index in range(4):
            two_heads = jnp.concatenate(
                [
                    jnp.where(head_of == 2 * index, pair_queries, nothing),
                    jnp.where(head_of == 2 * index + 1, pair_queries, nothing),
                ],
                axis=1,
            )
            scores[pair, index] = dot_nn(pair_keys, two_heads)
        return carry

    lax.fori_loop(0, 4, score, 0)

    def soft(values, bias):
        values = values + bias
        low, high = values[:128], values[128:]
        top_low = jnp.max(low, axis=0, keepdims=True)
        top_high = jnp.max(high, axis=0, keepdims=True)
        return jnp.concatenate(
            [
                jnp.exp(low - jnp.maximum(top_low, top_high + gap)),
                jnp.exp(high - jnp.maximum(top_low - gap, top_high)),
            ],
            axis=0,
        ).astype(BF16)

    def pair_of(step):
        return templ ^ (3 - step ^ (1 - step // 2))

    def finish(step):
        pair = pair_of(step)
        projected = dot_tn(gated[pair], w_tri)
        result = (rows_in[pair, mine, :].astype(F32) + projected).astype(BF16)
        fresh[pair] = result

        @pl.when(step == 3)
        def _():
            peers_in[templ] = result

        @pl.when(step < 3)
        def _():
            pltpu.make_async_remote_copy(
                src_ref=fresh.at[pair],
                dst_ref=peers_in.at[templ],
                send_sem=peer_send.at[step],
                recv_sem=peer_recv.at[templ],
                device_id=(pair, row, col),
                device_id_type=MESH,
            ).start()

    def attend(count, carry):
        heads, turn = count // 2, count % 2

        @pl.when(turn == 0)
        def _():
            drain(bias_in.at[heads], bias_recv.at[heads])
            first_half = iota((256, 128), 1) < 64
            one = bias_in[heads, 0].astype(F32)
            two = bias_in[heads, 1].astype(F32)
            bias_full[0] = jnp.where(first_half, one, pltpu.roll(two, 64, 1))
            bias_full[1] = jnp.where(first_half, pltpu.roll(one, 64, 1), two)

        for step in (2 * turn, 2 * turn + 1):
            pair = pair_of(step)
            for side in range(2):
                both = scores[pair, 2 * side + heads]
                weights = jnp.concatenate(
                    [soft(both[:, :128], bias_full[0]), soft(both[:, 128:], bias_full[1])], axis=1
                )
                place = pl.ds(pl.multiple_of(64 * side + 32 * heads, 32), 32)
                mixed = dot_nn(jnp.concatenate([values[pair, place, :], ones_rows], axis=0), weights)
                attended = jnp.concatenate(
                    [mixed[:16, :128] / mixed[32:, :128], mixed[16:32, 128:] / mixed[32:, 128:]], axis=0
                )
                gated[pair, place, :] = (attended * gates[pair, place, :]).astype(BF16)

            @pl.when(heads == 1)
            def _(step=step):
                finish(step)

        return carry

    lax.fori_loop(0, 4, attend, 0)

    new_place = new_out.at[pl.ds(4 * chunk, 4)]

    def returned(to_chunk):
        return fresh.at[:, pl.ds(pl.multiple_of(16 * to_chunk, 16), 16), :]

    def send_new(step, carry):
        to_chunk = (chunk + step) % 8
        pltpu.make_async_remote_copy(
            src_ref=returned(to_chunk),
            dst_ref=new_place,
            send_sem=new_send,
            recv_sem=new_recv,
            device_id=(templ, row, 8 * half + to_chunk),
            device_id_type=MESH,
        ).start()
        return carry

    lax.fori_loop(1, 8, send_new, 0)
    pltpu.make_async_copy(returned(chunk), new_place, new_recv).start()

    pltpu.make_async_copy(main_in, main_in, main_recv).wait()
    main_query = 0.25 * (
        dot_nt(main_in[0], jnp.concatenate([w_query, nothing], axis=0))
        + dot_nt(main_in[1], jnp.concatenate([nothing, w_query], axis=0))
    )

    def prepare(first, second):
        both = jnp.concatenate([peers_in[first], peers_in[second]], axis=0)
        both_normed = pair_norm(both, averager, merge_gain)
        merge_keys = dot_nn(both_normed, w_merge_key).astype(BF16).astype(F32)
        both_shown = dot_nn(both_normed, w_merge_value).astype(BF16).astype(F32)
        products = split_dot(jnp.concatenate([main_query, main_query], axis=0) * merge_keys, summer)
        for index, other in enumerate((first, second)):
            valid = coverage_ref[row_block, other] * coverage_ref[half, other] * mask_ref[row_block, half]
            part = slice(128 * index, 128 * index + 128)
            merge_scores.append(products[part] + MASK_SHIFT * (valid.astype(F32) - 1.0))
            shown.append(both_shown[part])

    merge_scores = []
    shown = []
    drain(peers_in.at[templ ^ 1], peer_recv.at[templ ^ 1])
    prepare(templ, templ ^ 1)
    for other in (templ ^ 2, templ ^ 3):
        drain(peers_in.at[other], peer_recv.at[other])
    prepare(templ ^ 2, templ ^ 3)
    highest = jnp.maximum(
        jnp.maximum(merge_scores[0], merge_scores[1]), jnp.maximum(merge_scores[2], merge_scores[3])
    )
    weights = [jnp.exp(one - highest) for one in merge_scores]
    total = (weights[0] + weights[1]) + (weights[2] + weights[3])
    blend = (weights[0] * shown[0] + weights[1] * shown[1]) + (weights[2] * shown[2] + weights[3] * shown[3])
    merged[...] = (blend / total).astype(BF16)

    pltpu.make_async_copy(
        merged.at[pl.ds(pl.multiple_of(16 * chunk, 16), 16), :],
        merged_out.at[4 * chunk + templ],
        merged_recv,
    ).start()

    pl.semaphore_wait(second_sem, 3)

    def send_merged(step, carry):
        to_templ, to_chunk = templ ^ (3 - step // 8), (chunk + 4 + step) % 8

        @pl.when((to_templ != templ) | (to_chunk != chunk))
        def _():
            pltpu.make_async_remote_copy(
                src_ref=merged.at[pl.ds(pl.multiple_of(16 * to_chunk, 16), 16), :],
                dst_ref=merged_out.at[4 * chunk + templ],
                send_sem=merged_send,
                recv_sem=merged_recv,
                device_id=(to_templ, row, 8 * half + to_chunk),
                device_id_type=MESH,
            ).start()

        return carry

    lax.fori_loop(0, 32, send_merged, 0)

    for step in range(3):
        drain(fresh.at[0], peer_send.at[step])
    drain(sizes.at[pl.ds(0, 30)], rows_send)
    drain(sizes.at[pl.ds(0, 3)], cross_send)
    for heads in range(2):
        drain(sizes.at[pl.ds(0, 15)], bias_send.at[heads])
    drain(sizes.at[pl.ds(0, 7)], main_send)
    drain(sizes.at[pl.ds(0, 14)], new_send)
    drain(packed.at[pl.ds(0, 31)], merged_send)
    drain(new_out, new_recv)
    drain(merged_out, merged_recv)


def out_kernel(new_ref, merged_ref, w_out_ref, templ_ref, embedding_ref):
    new = new_ref[...]
    templ_ref[0, pl.ds(0, 32)] = new[:, :, :64]
    templ_ref[0, pl.ds(32, 32)] = new[:, :, 64:]
    merged = merged_ref[...].reshape(512, 128)
    w_out = w_out_ref[...]
    nothing = jnp.zeros_like(w_out)
    first = dot_nn(merged, jnp.concatenate([w_out, nothing], axis=0))
    second = dot_nn(merged, jnp.concatenate([nothing, w_out], axis=0))
    embedding_ref[pl.ds(0, 32)] = first.astype(BF16).reshape(32, 16, 128)
    embedding_ref[pl.ds(32, 32)] = second.astype(BF16).reshape(32, 16, 128)


def on_device(
    templ_pair,
    main_pair,
    coverage,
    pair_mask,
    tri_gain,
    w_project,
    w_bias,
    w_tri_out,
    merge_gain,
    w_merge_q,
    w_merge_kv,
    w_merge_out,
):
    vmem = pl.BlockSpec(memory_space=pltpu.VMEM)
    anywhere = pl.BlockSpec(memory_space=pl.ANY)
    piece = jax.ShapeDtypeStruct((32, 16, 128), BF16)
    dma = pltpu.SemaphoreType.DMA
    new, merged = pl.pallas_call(
        pair_kernel,
        out_shape=(piece, piece),
        in_specs=[pl.BlockSpec(memory_space=pltpu.HBM)] * 11,
        out_specs=(anywhere, anywhere),
        scratch_shapes=[
            pltpu.VMEM((64, 16, 64), BF16),
            pltpu.SMEM((2, 4), jnp.int32),
            pltpu.SMEM((2, 2), jnp.int32),
            pltpu.VMEM((1, 64), F32),
            pltpu.VMEM((64, 256), BF16),
            pltpu.VMEM((4, 64), BF16),
            pltpu.VMEM((64, 64), BF16),
            pltpu.VMEM((1, 64), F32),
            pltpu.VMEM((64, 128), BF16),
            pltpu.VMEM((64, 128), BF16),
            pltpu.VMEM((32, 16, 128), BF16),
            pltpu.VMEM((4, 256, 128), BF16),
            pltpu.VMEM((2, 4, 16, 128), BF16),
            pltpu.VMEM((2, 2, 256, 128), BF16),
            pltpu.VMEM((2, 256, 128), F32),
            pltpu.VMEM((2, 128, 128), BF16),
            pltpu.VMEM((4, 256, 128), BF16),
            pltpu.VMEM((4, 256, 128), BF16),
            pltpu.VMEM((4, 128, 256), BF16),
            pltpu.VMEM((4, 128, 128), BF16),
            pltpu.VMEM((4, 128, 128), F32),
            pltpu.VMEM((4, 4, 256, 256), F32),
            pltpu.VMEM((4, 128, 128), BF16),
            pltpu.VMEM((4, 128, 128), BF16),
            pltpu.VMEM((4, 128, 128), BF16),
            pltpu.VMEM((128, 128), BF16),
            pltpu.VMEM((32, 16, 256), BF16),
            dma((10,)),
            dma,
            dma,
            dma,
            dma,
            dma((2,)),
            dma((2,)),
            dma,
            dma,
            dma((4,)),
            dma((4,)),
            dma,
            dma,
            dma,
            dma,
            pltpu.SemaphoreType.REGULAR,
        ],
        compiler_params=pltpu.CompilerParams(
            collective_id=0, has_side_effects=True, vmem_limit_bytes=64 * 1024 * 1024
        ),
        name="pair_kernel",
    )(
        templ_pair[0],
        main_pair.reshape(2, 32, 16, 128),
        coverage.T,
        pair_mask,
        tri_gain.reshape(1, 64),
        w_project,
        w_bias.T,
        w_tri_out,
        merge_gain.reshape(1, 64),
        w_merge_q.T,
        w_merge_kv,
    )
    return pl.pallas_call(
        out_kernel,
        out_shape=(
            jax.ShapeDtypeStruct((1, 64, 16, 64), BF16),
            jax.ShapeDtypeStruct((64, 16, 128), BF16),
        ),
        in_specs=[vmem] * 3,
        out_specs=(vmem, vmem),
        compiler_params=pltpu.CompilerParams(vmem_limit_bytes=64 * 1024 * 1024),
        name="out_kernel",
    )(new, merged, w_merge_out)


def solution(mesh):
    whole = P()
    tiles = P("tmpl", "row", "col", None)
    pairs = P("row", "col", None)
    return jax.shard_map(
        on_device,
        mesh=mesh,
        in_specs=(tiles, pairs) + (whole,) * 10,
        out_specs=(tiles, pairs),
        check_vma=False,
    )
```

```python
import jax
import jax.numpy as jnp
from jax import lax
from jax.experimental import pallas as pl
from jax.experimental.pallas import tpu as pltpu
from jax.sharding import PartitionSpec as P

MASK_SHIFT = 10000.0
EPSILON = 1e-05
MESH = pl.DeviceIdType.MESH
F32 = jnp.float32
BF16 = jnp.bfloat16


def iota(shape, axis):
    return lax.broadcasted_iota(jnp.int32, shape, axis)


def dot_nn(a, b):
    return lax.dot_general(a, b, (((1,), (0,)), ((), ())), preferred_element_type=F32)


def dot_nt(a, b):
    return lax.dot_general(a, b, (((1,), (1,)), ((), ())), preferred_element_type=F32)


def dot_tn(a, b):
    return lax.dot_general(a, b, (((0,), (0,)), ((), ())), preferred_element_type=F32)


def split_dot(values, weights):
    high = values.astype(BF16)
    low = (values - high.astype(F32)).astype(BF16)
    return dot_nn(high, weights) + dot_nn(low, weights)


def pair_norm(values, averager, gain):
    center = values.astype(F32) - dot_nn(values, averager)
    spread = split_dot(center * center, averager)
    return (center * lax.rsqrt(spread + EPSILON) * gain).astype(BF16)


def ones_where(condition):
    return jnp.where(condition, 1.0, 0.0).astype(BF16)


def diagonal(doubled):
    both = jnp.concatenate([doubled, doubled], axis=0)
    keep = (iota((128, 128), 0) < 64) == (iota((128, 128), 1) < 64)
    return jnp.where(keep, both, 0.0).astype(BF16)


def pick_columns(width, first):
    return ones_where(iota((width, 128), 0) == first + iota((width, 128), 1) % 64)


def pair_kernel(
    templ_hbm,
    main_hbm,
    coverage_hbm,
    mask_hbm,
    tri_gain_hbm,
    w_project_hbm,
    w_bias_hbm,
    w_tri_hbm,
    merge_gain_hbm,
    w_query_hbm,
    w_kv_hbm,
    new_out,
    merged_out,
    tile,
    coverage_ref,
    mask_ref,
    tri_gain_ref,
    w_project_ref,
    w_bias_ref,
    w_tri_ref,
    merge_gain_ref,
    w_query_ref,
    w_kv_ref,
    packed,
    rows_in,
    bias_rows,
    bias_in,
    bias_full,
    main_in,
    normed,
    keys,
    values,
    queries,
    gates,
    scores,
    gated,
    fresh,
    peers_in,
    merged,
    sizes,
    load_sem,
    rows_send,
    rows_recv,
    cross_send,
    cross_recv,
    bias_send,
    bias_recv,
    main_send,
    main_recv,
    peer_send,
    peer_recv,
    new_send,
    new_recv,
    merged_send,
    merged_recv,
    second_sem,
):
    templ = lax.axis_index("tmpl")
    row = lax.axis_index("row")
    col = lax.axis_index("col")
    plane = col // 2
    half, chunk = col // 8, col % 8
    own_cols = pl.ds(pl.multiple_of(16 * col, 16), 16)

    loads = [
        pltpu.make_async_copy(source, target, load_sem.at[index])
        for index, (source, target) in enumerate(
            (
                (templ_hbm, tile),
                (tri_gain_hbm, tri_gain_ref),
                (w_bias_hbm, w_bias_ref),
                (w_project_hbm, w_project_ref),
                (w_tri_hbm, w_tri_ref),
                (merge_gain_hbm, merge_gain_ref),
                (w_query_hbm, w_query_ref),
                (w_kv_hbm, w_kv_ref),
                (coverage_hbm, coverage_ref),
                (mask_hbm, mask_ref),
            )
        )
    ]
    loads[0].start()
    barrier = pltpu.get_barrier_semaphore()
    for step in (8, 9, 7, 10, 6, 11, 5, 12, 4, 13, 3, 14, 2, 15, 1):
        pl.semaphore_signal(barrier, inc=1, device_id=(templ, row, (col + step) % 16), device_id_type=MESH)
    for step in range(1, 4):
        pl.semaphore_signal(barrier, inc=1, device_id=(templ, (row + step) % 4, col), device_id_type=MESH)
        pl.semaphore_signal(barrier, inc=1, device_id=((templ + step) % 4, row, col), device_id_type=MESH)
    for load in loads[1:]:
        load.start()

    for load in loads[:3]:
        load.wait()
    eye = iota((64, 128), 0)
    lane = iota((64, 128), 1)
    low_rows = tile[pl.ds(0, 32)].reshape(512, 64)
    high_rows = tile[pl.ds(32, 32)].reshape(512, 64)
    together = dot_nn(low_rows, ones_where(eye == lane)) + dot_nn(high_rows, ones_where(eye + 64 == lane))
    packed[...] = together.astype(BF16).reshape(32, 16, 128)

    averager = jnp.where(
        (iota((128, 128), 0) < 64) == (iota((128, 128), 1) < 64), 1.0 / 64, 0.0
    ).astype(BF16)
    tri_gain = jnp.concatenate([tri_gain_ref[...], tri_gain_ref[...]], axis=1)

    own_normed = pair_norm(packed[...].reshape(512, 128), averager, tri_gain)
    w_bias = dot_nn(w_bias_ref[...], pick_columns(64, 0))
    which = iota((256, 128), 0)
    spread_bias = jnp.zeros((256, 128), F32)
    for head in range(4):
        spread_bias = jnp.where(which // 64 == head, w_bias[head : head + 1, :], spread_bias)
    spread_bias = jnp.where((which // 32) % 2 == iota((256, 128), 1) // 64, spread_bias, 0.0).astype(BF16)
    every_bias = dot_nt(own_normed, spread_bias).reshape(32, 16, 256)
    place = iota((16, 256), 1) % 32
    chosen = jnp.zeros((16, 256), F32)
    for index in range(32):
        chosen = jnp.where(place == index, every_bias[index], chosen)
    chosen = chosen.astype(BF16)
    bias_rows[0, row] = chosen[:, :128]
    bias_rows[1, row] = chosen[:, 128:]

    pl.semaphore_wait(barrier, 21)
    for step in range(1, 4):
        pl.semaphore_signal(second_sem, inc=1, device_id=((templ + step) % 4, row, col), device_id_type=MESH)

    def far_first(index):
        away = (index // 2 + 1) // 2 * (2 * (index // 2 % 2) - 1)
        return 2 * ((plane + 4 + away) % 8) + (col + index) % 2

    def send_to_columns(source_of, target, local_target, send_sem, recv_sem):
        def one(index, carry):
            to = far_first(index)
            pltpu.make_async_remote_copy(
                src_ref=source_of(to),
                dst_ref=target,
                send_sem=send_sem,
                recv_sem=recv_sem,
                device_id=(templ, row, to),
                device_id_type=MESH,
            ).start()
            return carry

        lax.fori_loop(0, 14, one, 0)
        one(15, 0)
        pltpu.make_async_copy(source_of(col), local_target, recv_sem).start()

    rows_place = rows_in.at[:, own_cols, :]
    send_to_columns(
        lambda to: packed.at[pl.ds(4 * (to % 8), 4)], rows_place, rows_place, rows_send, rows_recv
    )

    for step in range(1, 4):
        pltpu.make_async_remote_copy(
            src_ref=bias_rows.at[:, row],
            dst_ref=bias_rows.at[:, row],
            send_sem=cross_send,
            recv_sem=cross_recv,
            device_id=(templ, (row + step) % 4, col),
            device_id_type=MESH,
        ).start()

    for load in loads[3:]:
        load.wait()
    w_project = w_project_ref[...]
    double = pick_columns(64, 0)

    def turned(first):
        columns = ones_where(iota((128, 256), 1) == first + iota((128, 256), 0) % 64)
        wide = dot_nn(dot_nt(columns, w_project).astype(BF16), double)
        keep = (iota((128, 128), 0) < 64) == (iota((128, 128), 1) < 64)
        return jnp.where(keep, wide, 0.0).astype(BF16)

    turned_query, turned_value, turned_gate = turned(0), turned(128), turned(192)
    w_key = diagonal(dot_nn(w_project, pick_columns(256, 64)))
    w_tri = diagonal(dot_nn(w_tri_ref[...], double))
    ones_rows = jnp.ones((16, 256), BF16)
    head_of = iota((128, 128), 0) // 16

    w_query = w_query_ref[...]
    nothing = jnp.zeros_like(w_query)
    w_kv = w_kv_ref[...]
    w_merge_key = diagonal(dot_nn(w_kv, pick_columns(128, 0)))
    w_merge_value = diagonal(dot_nn(w_kv, pick_columns(128, 64)))
    merge_gain = jnp.concatenate([merge_gain_ref[...], merge_gain_ref[...]], axis=1)
    summer = ones_where(iota((128, 128), 0) // 16 == iota((128, 128), 1) // 16)

    def drain(ref, sem):
        pltpu.make_async_copy(ref, ref, sem).wait()

    drain(sizes.at[pl.ds(0, 3)], cross_recv)
    for heads in range(2):
        bias_place = bias_in.at[heads, :, own_cols, :]
        send_to_columns(
            lambda to, heads=heads: bias_rows.at[heads, pl.ds(2 * (to // 8), 2)],
            bias_place,
            bias_place,
            bias_send.at[heads],
            bias_recv.at[heads],
        )

    main_place = main_in.at[:, pl.ds(pl.multiple_of(16 * chunk, 16), 16), :]
    pltpu.make_async_copy(main_hbm.at[:, 4 * chunk + templ], main_place, main_recv).start()

    def send_main(step, carry):
        to_chunk = (chunk + step) % 8
        pltpu.make_async_remote_copy(
            src_ref=main_hbm.at[:, 4 * to_chunk + templ],
            dst_ref=main_place,
            send_sem=main_send,
            recv_sem=main_recv,
            device_id=(templ, row, 8 * half + to_chunk),
            device_id_type=MESH,
        ).start()
        return carry

    lax.fori_loop(1, 8, send_main, 0)

    row_block = row // 2
    cover_row = coverage_ref[row_block, templ]
    shift_low = MASK_SHIFT * ((cover_row * coverage_ref[0, templ] * mask_ref[row_block, 0]).astype(F32) - 1.0)
    shift_high = MASK_SHIFT * ((cover_row * coverage_ref[1, templ] * mask_ref[row_block, 1]).astype(F32) - 1.0)
    gap = shift_high - shift_low
    mine = pl.ds(pl.multiple_of(128 * half, 128), 128)

    drain(rows_in, rows_recv)
    every_normed = pair_norm(rows_in[...].reshape(1024, 128), averager, tri_gain)
    normed[...] = every_normed.reshape(4, 256, 128)
    keys[...] = dot_nn(every_normed, w_key).astype(BF16).reshape(4, 256, 128)
    every_value = dot_nt(turned_value, every_normed).astype(BF16)
    own_part = normed[:, mine, :].reshape(512, 128)
    every_query = (dot_nt(turned_query, own_part) * 0.25).astype(BF16)
    every_gate = jax.nn.sigmoid(dot_nt(turned_gate, own_part))
    for pair in range(4):
        values[pair] = every_value[:, 256 * pair : 256 * pair + 256]
        queries[pair] = every_query[:, 128 * pair : 128 * pair + 128]
        gates[pair] = every_gate[:, 128 * pair : 128 * pair + 128]

    def score(pair, carry):
        pair_keys, pair_queries = keys[pair], queries[pair]
        nothing = jnp.zeros_like(pair_queries)
        for index in range(4):
            two_heads = jnp.concatenate(
                [
                    jnp.where(head_of == 2 * index, pair_queries, nothing),
                    jnp.where(head_of == 2 * index + 1, pair_queries, nothing),
                ],
                axis=1,
            )
            scores[pair, index] = dot_nn(pair_keys, two_heads)
        return carry

    lax.fori_loop(0, 4, score, 0)

    def soft(values, bias):
        values = values + bias
        low, high = values[:128], values[128:]
        top_low = jnp.max(low, axis=0, keepdims=True)
        top_high = jnp.max(high, axis=0, keepdims=True)
        return jnp.concatenate(
            [
                jnp.exp(low - jnp.maximum(top_low, top_high + gap)),
                jnp.exp(high - jnp.maximum(top_low - gap, top_high)),
            ],
            axis=0,
        ).astype(BF16)

    def pair_of(step):
        return templ ^ (3 - step ^ (1 - step // 2))

    def finish(step):
        pair = pair_of(step)
        projected = dot_tn(gated[pair], w_tri)
        result = (rows_in[pair, mine, :].astype(F32) + projected).astype(BF16)
        fresh[pair] = result

        @pl.when(step == 3)
        def _():
            peers_in[templ] = result

        @pl.when(step < 3)
        def _():
            pltpu.make_async_remote_copy(
                src_ref=fresh.at[pair],
                dst_ref=peers_in.at[templ],
                send_sem=peer_send.at[step],
                recv_sem=peer_recv.at[templ],
                device_id=(pair, row, col),
                device_id_type=MESH,
            ).start()

    def attend(count, carry):
        heads, turn = count // 2, count % 2

        @pl.when(turn == 0)
        def _():
            drain(bias_in.at[heads], bias_recv.at[heads])
            first_half = iota((256, 128), 1) < 64
            one = bias_in[heads, 0].astype(F32)
            two = bias_in[heads, 1].astype(F32)
            bias_full[0] = jnp.where(first_half, one, pltpu.roll(two, 64, 1))
            bias_full[1] = jnp.where(first_half, pltpu.roll(one, 64, 1), two)

        for step in (2 * turn, 2 * turn + 1):
            pair = pair_of(step)
            for side in range(2):
                both = scores[pair, 2 * side + heads]
                weights = jnp.concatenate(
                    [soft(both[:, :128], bias_full[0]), soft(both[:, 128:], bias_full[1])], axis=1
                )
                place = pl.ds(pl.multiple_of(64 * side + 32 * heads, 32), 32)
                mixed = dot_nn(jnp.concatenate([values[pair, place, :], ones_rows], axis=0), weights)
                attended = jnp.concatenate(
                    [mixed[:16, :128] / mixed[32:, :128], mixed[16:32, 128:] / mixed[32:, 128:]], axis=0
                )
                gated[pair, place, :] = (attended * gates[pair, place, :]).astype(BF16)

            @pl.when(heads == 1)
            def _(step=step):
                finish(step)

        return carry

    lax.fori_loop(0, 4, attend, 0)

    new_place = new_out.at[pl.ds(4 * chunk, 4)]

    def returned(to_chunk):
        return fresh.at[:, pl.ds(pl.multiple_of(16 * to_chunk, 16), 16), :]

    def send_new(step, carry):
        to_chunk = (chunk + step) % 8
        pltpu.make_async_remote_copy(
            src_ref=returned(to_chunk),
            dst_ref=new_place,
            send_sem=new_send,
            recv_sem=new_recv,
            device_id=(templ, row, 8 * half + to_chunk),
            device_id_type=MESH,
        ).start()
        return carry

    lax.fori_loop(1, 8, send_new, 0)
    pltpu.make_async_copy(returned(chunk), new_place, new_recv).start()

    pltpu.make_async_copy(main_in, main_in, main_recv).wait()
    main_query = 0.25 * (
        dot_nt(main_in[0], jnp.concatenate([w_query, nothing], axis=0))
        + dot_nt(main_in[1], jnp.concatenate([nothing, w_query], axis=0))
    )

    def prepare(first, second):
        both = jnp.concatenate([peers_in[first], peers_in[second]], axis=0)
        both_normed = pair_norm(both, averager, merge_gain)
        merge_keys = dot_nn(both_normed, w_merge_key).astype(BF16).astype(F32)
        both_shown = dot_nn(both_normed, w_merge_value).astype(BF16).astype(F32)
        products = split_dot(jnp.concatenate([main_query, main_query], axis=0) * merge_keys, summer)
        for index, other in enumerate((first, second)):
            valid = coverage_ref[row_block, other] * coverage_ref[half, other] * mask_ref[row_block, half]
            part = slice(128 * index, 128 * index + 128)
            merge_scores.append(products[part] + MASK_SHIFT * (valid.astype(F32) - 1.0))
            shown.append(both_shown[part])

    merge_scores = []
    shown = []
    drain(peers_in.at[templ ^ 1], peer_recv.at[templ ^ 1])
    prepare(templ, templ ^ 1)
    for other in (templ ^ 2, templ ^ 3):
        drain(peers_in.at[other], peer_recv.at[other])
    prepare(templ ^ 2, templ ^ 3)
    highest = jnp.maximum(
        jnp.maximum(merge_scores[0], merge_scores[1]), jnp.maximum(merge_scores[2], merge_scores[3])
    )
    weights = [jnp.exp(one - highest) for one in merge_scores]
    total = (weights[0] + weights[1]) + (weights[2] + weights[3])
    blend = (weights[0] * shown[0] + weights[1] * shown[1]) + (weights[2] * shown[2] + weights[3] * shown[3])
    merged[...] = (blend / total).astype(BF16)

    pltpu.make_async_copy(
        merged.at[pl.ds(pl.multiple_of(16 * chunk, 16), 16), :],
        merged_out.at[4 * chunk + templ],
        merged_recv,
    ).start()

    pl.semaphore_wait(second_sem, 3)

    def send_merged(step, carry):
        to_templ, to_chunk = templ ^ (3 - step // 8), (chunk + 4 + step) % 8

        @pl.when((to_templ != templ) | (to_chunk != chunk))
        def _():
            pltpu.make_async_remote_copy(
                src_ref=merged.at[pl.ds(pl.multiple_of(16 * to_chunk, 16), 16), :],
                dst_ref=merged_out.at[4 * chunk + templ],
                send_sem=merged_send,
                recv_sem=merged_recv,
                device_id=(to_templ, row, 8 * half + to_chunk),
                device_id_type=MESH,
            ).start()

        return carry

    lax.fori_loop(0, 32, send_merged, 0)

    for step in range(3):
        drain(fresh.at[0], peer_send.at[step])
    drain(sizes.at[pl.ds(0, 30)], rows_send)
    drain(sizes.at[pl.ds(0, 3)], cross_send)
    for heads in range(2):
        drain(sizes.at[pl.ds(0, 15)], bias_send.at[heads])
    drain(sizes.at[pl.ds(0, 7)], main_send)
    drain(sizes.at[pl.ds(0, 14)], new_send)
    drain(packed.at[pl.ds(0, 31)], merged_send)
    drain(new_out, new_recv)
    drain(merged_out, merged_recv)


def out_kernel(new_ref, merged_ref, w_out_ref, templ_ref, embedding_ref):
    new = new_ref[...]
    templ_ref[0, pl.ds(0, 32)] = new[:, :, :64]
    templ_ref[0, pl.ds(32, 32)] = new[:, :, 64:]
    merged = merged_ref[...].reshape(512, 128)
    w_out = w_out_ref[...]
    nothing = jnp.zeros_like(w_out)
    first = dot_nn(merged, jnp.concatenate([w_out, nothing], axis=0))
    second = dot_nn(merged, jnp.concatenate([nothing, w_out], axis=0))
    embedding_ref[pl.ds(0, 32)] = first.astype(BF16).reshape(32, 16, 128)
    embedding_ref[pl.ds(32, 32)] = second.astype(BF16).reshape(32, 16, 128)


def on_device(
    templ_pair,
    main_pair,
    coverage,
    pair_mask,
    tri_gain,
    w_project,
    w_bias,
    w_tri_out,
    merge_gain,
    w_merge_q,
    w_merge_kv,
    w_merge_out,
):
    vmem = pl.BlockSpec(memory_space=pltpu.VMEM)
    anywhere = pl.BlockSpec(memory_space=pl.ANY)
    piece = jax.ShapeDtypeStruct((32, 16, 128), BF16)
    dma = pltpu.SemaphoreType.DMA
    new, merged = pl.pallas_call(
        pair_kernel,
        out_shape=(piece, piece),
        in_specs=[pl.BlockSpec(memory_space=pltpu.HBM)] * 11,
        out_specs=(anywhere, anywhere),
        scratch_shapes=[
            pltpu.VMEM((64, 16, 64), BF16),
            pltpu.SMEM((2, 4), jnp.int32),
            pltpu.SMEM((2, 2), jnp.int32),
            pltpu.VMEM((1, 64), F32),
            pltpu.VMEM((64, 256), BF16),
            pltpu.VMEM((4, 64), BF16),
            pltpu.VMEM((64, 64), BF16),
            pltpu.VMEM((1, 64), F32),
            pltpu.VMEM((64, 128), BF16),
            pltpu.VMEM((64, 128), BF16),
            pltpu.VMEM((32, 16, 128), BF16),
            pltpu.VMEM((4, 256, 128), BF16),
            pltpu.VMEM((2, 4, 16, 128), BF16),
            pltpu.VMEM((2, 2, 256, 128), BF16),
            pltpu.VMEM((2, 256, 128), F32),
            pltpu.VMEM((2, 128, 128), BF16),
            pltpu.VMEM((4, 256, 128), BF16),
            pltpu.VMEM((4, 256, 128), BF16),
            pltpu.VMEM((4, 128, 256), BF16),
            pltpu.VMEM((4, 128, 128), BF16),
            pltpu.VMEM((4, 128, 128), F32),
            pltpu.VMEM((4, 4, 256, 256), F32),
            pltpu.VMEM((4, 128, 128), BF16),
            pltpu.VMEM((4, 128, 128), BF16),
            pltpu.VMEM((4, 128, 128), BF16),
            pltpu.VMEM((128, 128), BF16),
            pltpu.VMEM((32, 16, 256), BF16),
            dma((10,)),
            dma,
            dma,
            dma,
            dma,
            dma((2,)),
            dma((2,)),
            dma,
            dma,
            dma((4,)),
            dma((4,)),
            dma,
            dma,
            dma,
            dma,
            pltpu.SemaphoreType.REGULAR,
        ],
        compiler_params=pltpu.CompilerParams(
            collective_id=0, has_side_effects=True, vmem_limit_bytes=64 * 1024 * 1024
        ),
        name="pair_kernel",
    )(
        templ_pair[0],
        main_pair.reshape(2, 32, 16, 128),
        coverage.T,
        pair_mask,
        tri_gain.reshape(1, 64),
        w_project,
        w_bias.T,
        w_tri_out,
        merge_gain.reshape(1, 64),
        w_merge_q.T,
        w_merge_kv,
    )
    return pl.pallas_call(
        out_kernel,
        out_shape=(
            jax.ShapeDtypeStruct((1, 64, 16, 64), BF16),
            jax.ShapeDtypeStruct((64, 16, 128), BF16),
        ),
        in_specs=[vmem] * 3,
        out_specs=(vmem, vmem),
        compiler_params=pltpu.CompilerParams(vmem_limit_bytes=64 * 1024 * 1024),
        name="out_kernel",
    )(new, merged, w_merge_out)


def solution(mesh):
    whole = P()
    tiles = P("tmpl", "row", "col", None)
    pairs = P("row", "col", None)
    return jax.shard_map(
        on_device,
        mesh=mesh,
        in_specs=(tiles, pairs) + (whole,) * 10,
        out_specs=(tiles, pairs),
        check_vma=False,
    )
```

```python
import jax
import jax.numpy as jnp
from jax import lax
from jax.experimental import pallas as pl
from jax.experimental.pallas import tpu as pltpu
from jax.sharding import PartitionSpec as P

MASK_SHIFT = 10000.0
EPSILON = 1e-05
MESH = pl.DeviceIdType.MESH
F32 = jnp.float32
BF16 = jnp.bfloat16


def iota(shape, axis):
    return lax.broadcasted_iota(jnp.int32, shape, axis)


def dot_nn(a, b):
    return lax.dot_general(a, b, (((1,), (0,)), ((), ())), preferred_element_type=F32)


def dot_nt(a, b):
    return lax.dot_general(a, b, (((1,), (1,)), ((), ())), preferred_element_type=F32)


def dot_tn(a, b):
    return lax.dot_general(a, b, (((0,), (0,)), ((), ())), preferred_element_type=F32)


def split_dot(values, weights):
    high = values.astype(BF16)
    low = (values - high.astype(F32)).astype(BF16)
    return dot_nn(high, weights) + dot_nn(low, weights)


def pair_norm(values, averager, gain):
    center = values.astype(F32) - dot_nn(values, averager)
    spread = split_dot(center * center, averager)
    return (center * lax.rsqrt(spread + EPSILON) * gain).astype(BF16)


def ones_where(condition):
    return jnp.where(condition, 1.0, 0.0).astype(BF16)


def diagonal(doubled):
    both = jnp.concatenate([doubled, doubled], axis=0)
    keep = (iota((128, 128), 0) < 64) == (iota((128, 128), 1) < 64)
    return jnp.where(keep, both, 0.0).astype(BF16)


def pick_columns(width, first):
    return ones_where(iota((width, 128), 0) == first + iota((width, 128), 1) % 64)


def pair_kernel(
    templ_hbm,
    main_hbm,
    coverage_hbm,
    mask_hbm,
    tri_gain_hbm,
    w_project_hbm,
    w_bias_hbm,
    w_tri_hbm,
    merge_gain_hbm,
    w_query_hbm,
    w_kv_hbm,
    new_out,
    merged_out,
    tile,
    coverage_ref,
    mask_ref,
    tri_gain_ref,
    w_project_ref,
    w_bias_ref,
    w_tri_ref,
    merge_gain_ref,
    w_query_ref,
    w_kv_ref,
    packed,
    rows_in,
    bias_rows,
    bias_in,
    bias_full,
    main_in,
    normed,
    keys,
    values,
    queries,
    gates,
    scores,
    gated,
    fresh,
    peers_in,
    merged,
    sizes,
    load_sem,
    rows_send,
    rows_recv,
    cross_send,
    cross_recv,
    bias_send,
    bias_recv,
    main_send,
    main_recv,
    peer_send,
    peer_recv,
    new_send,
    new_recv,
    merged_send,
    merged_recv,
    second_sem,
):
    templ = lax.axis_index("tmpl")
    row = lax.axis_index("row")
    col = lax.axis_index("col")
    plane = col // 2
    half, chunk = col // 8, col % 8
    own_cols = pl.ds(pl.multiple_of(16 * col, 16), 16)

    loads = [
        pltpu.make_async_copy(source, target, load_sem.at[index])
        for index, (source, target) in enumerate(
            (
                (templ_hbm, tile),
                (tri_gain_hbm, tri_gain_ref),
                (w_bias_hbm, w_bias_ref),
                (w_project_hbm, w_project_ref),
                (w_tri_hbm, w_tri_ref),
                (merge_gain_hbm, merge_gain_ref),
                (w_query_hbm, w_query_ref),
                (w_kv_hbm, w_kv_ref),
                (coverage_hbm, coverage_ref),
                (mask_hbm, mask_ref),
            )
        )
    ]
    loads[0].start()
    barrier = pltpu.get_barrier_semaphore()
    for step in (8, 9, 7, 10, 6, 11, 5, 12, 4, 13, 3, 14, 2, 15, 1):
        pl.semaphore_signal(barrier, inc=1, device_id=(templ, row, (col + step) % 16), device_id_type=MESH)
    for step in range(1, 4):
        pl.semaphore_signal(barrier, inc=1, device_id=(templ, (row + step) % 4, col), device_id_type=MESH)
        pl.semaphore_signal(barrier, inc=1, device_id=((templ + step) % 4, row, col), device_id_type=MESH)
    for load in loads[1:]:
        load.start()

    for load in loads[:3]:
        load.wait()
    eye = iota((64, 128), 0)
    lane = iota((64, 128), 1)
    low_rows = tile[pl.ds(0, 32)].reshape(512, 64)
    high_rows = tile[pl.ds(32, 32)].reshape(512, 64)
    together = dot_nn(low_rows, ones_where(eye == lane)) + dot_nn(high_rows, ones_where(eye + 64 == lane))
    packed[...] = together.astype(BF16).reshape(32, 16, 128)

    averager = jnp.where(
        (iota((128, 128), 0) < 64) == (iota((128, 128), 1) < 64), 1.0 / 64, 0.0
    ).astype(BF16)
    tri_gain = jnp.concatenate([tri_gain_ref[...], tri_gain_ref[...]], axis=1)

    own_normed = pair_norm(packed[...].reshape(512, 128), averager, tri_gain)
    w_bias = dot_nn(w_bias_ref[...], pick_columns(64, 0))
    which = iota((256, 128), 0)
    spread_bias = jnp.zeros((256, 128), F32)
    for head in range(4):
        spread_bias = jnp.where(which // 64 == head, w_bias[head : head + 1, :], spread_bias)
    spread_bias = jnp.where((which // 32) % 2 == iota((256, 128), 1) // 64, spread_bias, 0.0).astype(BF16)
    every_bias = dot_nt(own_normed, spread_bias).reshape(32, 16, 256)
    place = iota((16, 256), 1) % 32
    chosen = jnp.zeros((16, 256), F32)
    for index in range(32):
        chosen = jnp.where(place == index, every_bias[index], chosen)
    chosen = chosen.astype(BF16)
    bias_rows[0, row] = chosen[:, :128]
    bias_rows[1, row] = chosen[:, 128:]

    pl.semaphore_wait(barrier, 21)
    for step in range(1, 4):
        pl.semaphore_signal(second_sem, inc=1, device_id=((templ + step) % 4, row, col), device_id_type=MESH)

    def far_first(index):
        away = (index // 2 + 1) // 2 * (2 * (index // 2 % 2) - 1)
        return 2 * ((plane + 4 + away) % 8) + (col + index) % 2

    def send_to_columns(source_of, target, local_target, send_sem, recv_sem):
        def one(index, carry):
            to = far_first(index)
            pltpu.make_async_remote_copy(
                src_ref=source_of(to),
                dst_ref=target,
                send_sem=send_sem,
                recv_sem=recv_sem,
                device_id=(templ, row, to),
                device_id_type=MESH,
            ).start()
            return carry

        lax.fori_loop(0, 14, one, 0)
        one(15, 0)
        pltpu.make_async_copy(source_of(col), local_target, recv_sem).start()

    rows_place = rows_in.at[:, own_cols, :]
    send_to_columns(
        lambda to: packed.at[pl.ds(4 * (to % 8), 4)], rows_place, rows_place, rows_send, rows_recv
    )

    for step in range(1, 4):
        pltpu.make_async_remote_copy(
            src_ref=bias_rows.at[:, row],
            dst_ref=bias_rows.at[:, row],
            send_sem=cross_send,
            recv_sem=cross_recv,
            device_id=(templ, (row + step) % 4, col),
            device_id_type=MESH,
        ).start()

    for load in loads[3:]:
        load.wait()
    w_project = w_project_ref[...]
    double = pick_columns(64, 0)

    def turned(first):
        columns = ones_where(iota((128, 256), 1) == first + iota((128, 256), 0) % 64)
        wide = dot_nn(dot_nt(columns, w_project).astype(BF16), double)
        keep = (iota((128, 128), 0) < 64) == (iota((128, 128), 1) < 64)
        return jnp.where(keep, wide, 0.0).astype(BF16)

    turned_query, turned_value, turned_gate = turned(0), turned(128), turned(192)
    w_key = diagonal(dot_nn(w_project, pick_columns(256, 64)))
    w_tri = diagonal(dot_nn(w_tri_ref[...], double))
    ones_rows = jnp.ones((16, 256), BF16)
    head_of = iota((128, 128), 0) // 16

    w_query = w_query_ref[...]
    nothing = jnp.zeros_like(w_query)
    w_kv = w_kv_ref[...]
    w_merge_key = diagonal(dot_nn(w_kv, pick_columns(128, 0)))
    w_merge_value = diagonal(dot_nn(w_kv, pick_columns(128, 64)))
    merge_gain = jnp.concatenate([merge_gain_ref[...], merge_gain_ref[...]], axis=1)
    summer = ones_where(iota((128, 128), 0) // 16 == iota((128, 128), 1) // 16)

    def drain(ref, sem):
        pltpu.make_async_copy(ref, ref, sem).wait()

    drain(sizes.at[pl.ds(0, 3)], cross_recv)
    for heads in range(2):
        bias_place = bias_in.at[heads, :, own_cols, :]
        send_to_columns(
            lambda to, heads=heads: bias_rows.at[heads, pl.ds(2 * (to // 8), 2)],
            bias_place,
            bias_place,
            bias_send.at[heads],
            bias_recv.at[heads],
        )

    main_place = main_in.at[:, pl.ds(pl.multiple_of(16 * chunk, 16), 16), :]
    pltpu.make_async_copy(main_hbm.at[:, 4 * chunk + templ], main_place, main_recv).start()

    def send_main(step, carry):
        to_chunk = (chunk + step) % 8
        pltpu.make_async_remote_copy(
            src_ref=main_hbm.at[:, 4 * to_chunk + templ],
            dst_ref=main_place,
            send_sem=main_send,
            recv_sem=main_recv,
            device_id=(templ, row, 8 * half + to_chunk),
            device_id_type=MESH,
        ).start()
        return carry

    lax.fori_loop(1, 8, send_main, 0)

    row_block = row // 2
    cover_row = coverage_ref[row_block, templ]
    shift_low = MASK_SHIFT * ((cover_row * coverage_ref[0, templ] * mask_ref[row_block, 0]).astype(F32) - 1.0)
    shift_high = MASK_SHIFT * ((cover_row * coverage_ref[1, templ] * mask_ref[row_block, 1]).astype(F32) - 1.0)
    gap = shift_high - shift_low
    mine = pl.ds(pl.multiple_of(128 * half, 128), 128)

    drain(rows_in, rows_recv)
    every_normed = pair_norm(rows_in[...].reshape(1024, 128), averager, tri_gain)
    normed[...] = every_normed.reshape(4, 256, 128)
    keys[...] = dot_nn(every_normed, w_key).astype(BF16).reshape(4, 256, 128)
    every_value = dot_nt(turned_value, every_normed).astype(BF16)
    own_part = normed[:, mine, :].reshape(512, 128)
    every_query = (dot_nt(turned_query, own_part) * 0.25).astype(BF16)
    every_gate = jax.nn.sigmoid(dot_nt(turned_gate, own_part))
    for pair in range(4):
        values[pair] = every_value[:, 256 * pair : 256 * pair + 256]
        queries[pair] = every_query[:, 128 * pair : 128 * pair + 128]
        gates[pair] = every_gate[:, 128 * pair : 128 * pair + 128]

    def score(pair, carry):
        pair_keys, pair_queries = keys[pair], queries[pair]
        nothing = jnp.zeros_like(pair_queries)
        for index in range(4):
            two_heads = jnp.concatenate(
                [
                    jnp.where(head_of == 2 * index, pair_queries, nothing),
                    jnp.where(head_of == 2 * index + 1, pair_queries, nothing),
                ],
                axis=1,
            )
            scores[pair, index] = dot_nn(pair_keys, two_heads)
        return carry

    lax.fori_loop(0, 4, score, 0)

    def soft(values, bias):
        values = values + bias
        low, high = values[:128], values[128:]
        top_low = jnp.max(low, axis=0, keepdims=True)
        top_high = jnp.max(high, axis=0, keepdims=True)
        return jnp.concatenate(
            [
                jnp.exp(low - jnp.maximum(top_low, top_high + gap)),
                jnp.exp(high - jnp.maximum(top_low - gap, top_high)),
            ],
            axis=0,
        ).astype(BF16)

    def pair_of(step):
        return templ ^ (3 - step ^ (1 - step // 2))

    def finish(step):
        pair = pair_of(step)
        projected = dot_tn(gated[pair], w_tri)
        result = (rows_in[pair, mine, :].astype(F32) + projected).astype(BF16)
        fresh[pair] = result

        @pl.when(step == 3)
        def _():
            peers_in[templ] = result

        @pl.when(step < 3)
        def _():
            pltpu.make_async_remote_copy(
                src_ref=fresh.at[pair],
                dst_ref=peers_in.at[templ],
                send_sem=peer_send.at[step],
                recv_sem=peer_recv.at[templ],
                device_id=(pair, row, col),
                device_id_type=MESH,
            ).start()

    def attend(count, carry):
        heads, turn = count // 2, count % 2

        @pl.when(turn == 0)
        def _():
            drain(bias_in.at[heads], bias_recv.at[heads])
            first_half = iota((256, 128), 1) < 64
            one = bias_in[heads, 0].astype(F32)
            two = bias_in[heads, 1].astype(F32)
            bias_full[0] = jnp.where(first_half, one, pltpu.roll(two, 64, 1))
            bias_full[1] = jnp.where(first_half, pltpu.roll(one, 64, 1), two)

        for step in (2 * turn, 2 * turn + 1):
            pair = pair_of(step)
            for side in range(2):
                both = scores[pair, 2 * side + heads]
                weights = jnp.concatenate(
                    [soft(both[:, :128], bias_full[0]), soft(both[:, 128:], bias_full[1])], axis=1
                )
                place = pl.ds(pl.multiple_of(64 * side + 32 * heads, 32), 32)
                mixed = dot_nn(jnp.concatenate([values[pair, place, :], ones_rows], axis=0), weights)
                attended = jnp.concatenate(
                    [mixed[:16, :128] / mixed[32:, :128], mixed[16:32, 128:] / mixed[32:, 128:]], axis=0
                )
                gated[pair, place, :] = (attended * gates[pair, place, :]).astype(BF16)

            @pl.when(heads == 1)
            def _(step=step):
                finish(step)

        return carry

    lax.fori_loop(0, 4, attend, 0)

    new_place = new_out.at[pl.ds(4 * chunk, 4)]

    def returned(to_chunk):
        return fresh.at[:, pl.ds(pl.multiple_of(16 * to_chunk, 16), 16), :]

    def send_new(step, carry):
        to_chunk = (chunk + step) % 8
        pltpu.make_async_remote_copy(
            src_ref=returned(to_chunk),
            dst_ref=new_place,
            send_sem=new_send,
            recv_sem=new_recv,
            device_id=(templ, row, 8 * half + to_chunk),
            device_id_type=MESH,
        ).start()
        return carry

    lax.fori_loop(1, 8, send_new, 0)
    pltpu.make_async_copy(returned(chunk), new_place, new_recv).start()

    pltpu.make_async_copy(main_in, main_in, main_recv).wait()
    main_query = 0.25 * (
        dot_nt(main_in[0], jnp.concatenate([w_query, nothing], axis=0))
        + dot_nt(main_in[1], jnp.concatenate([nothing, w_query], axis=0))
    )

    def prepare(first, second):
        both = jnp.concatenate([peers_in[first], peers_in[second]], axis=0)
        both_normed = pair_norm(both, averager, merge_gain)
        merge_keys = dot_nn(both_normed, w_merge_key).astype(BF16).astype(F32)
        both_shown = dot_nn(both_normed, w_merge_value).astype(BF16).astype(F32)
        products = split_dot(jnp.concatenate([main_query, main_query], axis=0) * merge_keys, summer)
        for index, other in enumerate((first, second)):
            valid = coverage_ref[row_block, other] * coverage_ref[half, other] * mask_ref[row_block, half]
            part = slice(128 * index, 128 * index + 128)
            merge_scores.append(products[part] + MASK_SHIFT * (valid.astype(F32) - 1.0))
            shown.append(both_shown[part])

    merge_scores = []
    shown = []
    drain(peers_in.at[templ ^ 1], peer_recv.at[templ ^ 1])
    prepare(templ, templ ^ 1)
    for other in (templ ^ 2, templ ^ 3):
        drain(peers_in.at[other], peer_recv.at[other])
    prepare(templ ^ 2, templ ^ 3)
    highest = jnp.maximum(
        jnp.maximum(merge_scores[0], merge_scores[1]), jnp.maximum(merge_scores[2], merge_scores[3])
    )
    weights = [jnp.exp(one - highest) for one in merge_scores]
    total = (weights[0] + weights[1]) + (weights[2] + weights[3])
    blend = (weights[0] * shown[0] + weights[1] * shown[1]) + (weights[2] * shown[2] + weights[3] * shown[3])
    merged[...] = (blend / total).astype(BF16)

    pltpu.make_async_copy(
        merged.at[pl.ds(pl.multiple_of(16 * chunk, 16), 16), :],
        merged_out.at[4 * chunk + templ],
        merged_recv,
    ).start()

    pl.semaphore_wait(second_sem, 3)

    for other in (3, 2, 1, 0):
        for away in (4, 5, 3, 6, 2, 7, 1, 0) if other else (4, 5, 3, 6, 2, 7, 1):
            to_chunk = (chunk + away) % 8
            pltpu.make_async_remote_copy(
                src_ref=merged.at[pl.ds(pl.multiple_of(16 * to_chunk, 16), 16), :],
                dst_ref=merged_out.at[4 * chunk + templ],
                send_sem=merged_send,
                recv_sem=merged_recv,
                device_id=(templ ^ other, row, 8 * half + to_chunk),
                device_id_type=MESH,
            ).start()

    for step in range(3):
        drain(fresh.at[0], peer_send.at[step])
    drain(sizes.at[pl.ds(0, 30)], rows_send)
    drain(sizes.at[pl.ds(0, 3)], cross_send)
    for heads in range(2):
        drain(sizes.at[pl.ds(0, 15)], bias_send.at[heads])
    drain(sizes.at[pl.ds(0, 7)], main_send)
    drain(sizes.at[pl.ds(0, 14)], new_send)
    drain(packed.at[pl.ds(0, 31)], merged_send)
    drain(new_out, new_recv)
    drain(merged_out, merged_recv)


def out_kernel(new_ref, merged_ref, w_out_ref, templ_ref, embedding_ref):
    new = new_ref[...]
    templ_ref[0, pl.ds(0, 32)] = new[:, :, :64]
    templ_ref[0, pl.ds(32, 32)] = new[:, :, 64:]
    merged = merged_ref[...].reshape(512, 128)
    w_out = w_out_ref[...]
    nothing = jnp.zeros_like(w_out)
    first = dot_nn(merged, jnp.concatenate([w_out, nothing], axis=0))
    second = dot_nn(merged, jnp.concatenate([nothing, w_out], axis=0))
    embedding_ref[pl.ds(0, 32)] = first.astype(BF16).reshape(32, 16, 128)
    embedding_ref[pl.ds(32, 32)] = second.astype(BF16).reshape(32, 16, 128)


def on_device(
    templ_pair,
    main_pair,
    coverage,
    pair_mask,
    tri_gain,
    w_project,
    w_bias,
    w_tri_out,
    merge_gain,
    w_merge_q,
    w_merge_kv,
    w_merge_out,
):
    vmem = pl.BlockSpec(memory_space=pltpu.VMEM)
    anywhere = pl.BlockSpec(memory_space=pl.ANY)
    piece = jax.ShapeDtypeStruct((32, 16, 128), BF16)
    dma = pltpu.SemaphoreType.DMA
    new, merged = pl.pallas_call(
        pair_kernel,
        out_shape=(piece, piece),
        in_specs=[pl.BlockSpec(memory_space=pltpu.HBM)] * 11,
        out_specs=(anywhere, anywhere),
        scratch_shapes=[
            pltpu.VMEM((64, 16, 64), BF16),
            pltpu.SMEM((2, 4), jnp.int32),
            pltpu.SMEM((2, 2), jnp.int32),
            pltpu.VMEM((1, 64), F32),
            pltpu.VMEM((64, 256), BF16),
            pltpu.VMEM((4, 64), BF16),
            pltpu.VMEM((64, 64), BF16),
            pltpu.VMEM((1, 64), F32),
            pltpu.VMEM((64, 128), BF16),
            pltpu.VMEM((64, 128), BF16),
            pltpu.VMEM((32, 16, 128), BF16),
            pltpu.VMEM((4, 256, 128), BF16),
            pltpu.VMEM((2, 4, 16, 128), BF16),
            pltpu.VMEM((2, 2, 256, 128), BF16),
            pltpu.VMEM((2, 256, 128), F32),
            pltpu.VMEM((2, 128, 128), BF16),
            pltpu.VMEM((4, 256, 128), BF16),
            pltpu.VMEM((4, 256, 128), BF16),
            pltpu.VMEM((4, 128, 256), BF16),
            pltpu.VMEM((4, 128, 128), BF16),
            pltpu.VMEM((4, 128, 128), F32),
            pltpu.VMEM((4, 4, 256, 256), F32),
            pltpu.VMEM((4, 128, 128), BF16),
            pltpu.VMEM((4, 128, 128), BF16),
            pltpu.VMEM((4, 128, 128), BF16),
            pltpu.VMEM((128, 128), BF16),
            pltpu.VMEM((32, 16, 256), BF16),
            dma((10,)),
            dma,
            dma,
            dma,
            dma,
            dma((2,)),
            dma((2,)),
            dma,
            dma,
            dma((4,)),
            dma((4,)),
            dma,
            dma,
            dma,
            dma,
            pltpu.SemaphoreType.REGULAR,
        ],
        compiler_params=pltpu.CompilerParams(
            collective_id=0, has_side_effects=True, vmem_limit_bytes=64 * 1024 * 1024
        ),
        name="pair_kernel",
    )(
        templ_pair[0],
        main_pair.reshape(2, 32, 16, 128),
        coverage.T,
        pair_mask,
        tri_gain.reshape(1, 64),
        w_project,
        w_bias.T,
        w_tri_out,
        merge_gain.reshape(1, 64),
        w_merge_q.T,
        w_merge_kv,
    )
    return pl.pallas_call(
        out_kernel,
        out_shape=(
            jax.ShapeDtypeStruct((1, 64, 16, 64), BF16),
            jax.ShapeDtypeStruct((64, 16, 128), BF16),
        ),
        in_specs=[vmem] * 3,
        out_specs=(vmem, vmem),
        compiler_params=pltpu.CompilerParams(vmem_limit_bytes=64 * 1024 * 1024),
        name="out_kernel",
    )(new, merged, w_merge_out)


def solution(mesh):
    whole = P()
    tiles = P("tmpl", "row", "col", None)
    pairs = P("row", "col", None)
    return jax.shard_map(
        on_device,
        mesh=mesh,
        in_specs=(tiles, pairs) + (whole,) * 10,
        out_specs=(tiles, pairs),
        check_vma=False,
    )
```
